32 devices in a mesh: shots: 2 (over x), xline: 8 (over z, y), inline: 2 (over core).
Axes of the slice: x: 2, y: 2, z: 4, core: 2. Of those that a mesh axis runs over, the one named last changes fastest.
Arguments:
- fwd_now: float32 [128, 64, 256], P(('shots', 'inline'), 'xline'), parts along dimension 0, may hold values from -6 to 6
- fwd_before: float32 [128, 64, 256], P(('shots', 'inline'), 'xline'), parts along dimension 0, may hold values from -6 to 6
- adj_now: float32 [128, 64, 256], P(('shots', 'inline'), 'xline'), parts along dimension 0, may hold values from -6 to 6
- adj_before: float32 [128, 64, 256], P(('shots', 'inline'), 'xline'), parts along dimension 0, may hold values from -6 to 6
- velocity: float32 [64, 64, 256], P('inline', 'xline'), may hold values from 0.2 to 0.4
- log_density: float32 [64, 64, 256], P('inline', 'xline'), may hold values from -0.3 to 0.3
- observed: float32 [16, 2048], P('shots', ('xline', 'inline')), parts along dimension 0, may hold values from -48 to 48
- rec_cells: int32 [16, 128], P(('xline', 'inline')), may hold values from 0 to 65535
- rec_counts: int32 [16, 16], P(('xline', 'inline')), may hold values from 0 to 8, as said below
- src_cell: int32 [32], P('shots'), parts along dimension 0, may hold values from 0 to 1048575
- wavelet: float32 [16, 16], P('shots'), parts along dimension 0, may hold values from -144 to 144
Outputs:
- gradient: float32 [512, 64, 64], P(('shots', 'xline'), 'inline'), parts along dimension 0
- adjoint_state: float32 [128, 64, 256], P(('shots', 'inline'), 'xline'), parts along dimension 0
- adjoint_previous: float32 [128, 64, 256], P(('shots', 'inline'), 'xline'), parts along dimension 0
The draws below stay inside these ranges and needn't reach their ends.
There are 2 independent parts, one for each index of `shots`. The reference program is written for one: setup_inputs(seed, part) draws one part's arguments, and reference() takes and returns one part's arrays. A program takes and returns all parts, laid end to end along the dimension named above; an argument that names none is the same for every part. Nothing has to cross between parts.
Inputs may be any that keep to these rules, and one draw needn't show every extreme that they name: rec_counts[o, s] live slots of the 8 that device s sends to subdomain o; in every draw one subdomain receives 8 live slots from every device.
All inputs are finite; a program needn't handle non-finite values.
Results may differ from the reference program's by a relative error of at most 0.04.
Values sent between devices are 32-bit elements; how exact they have to be, the bound alone decides.
A program may use at most 64 MiB of HBM per device.

```python
import jax
import jax.numpy as jnp
from jax import lax

CI = 32
CX = 8
NZ = 256
NT = 8
NSRC = 16
CAP = 8
NI = 64
NX = 64
SUBS = 16
SMOOTH = 16
N_INLINE = 2


def draw_rec_counts(key, part):
    key_top, key_raw, key_full = jax.random.split(key, 3)
    ceiling = jax.random.randint(key_top, (SUBS, 1), 1, CAP + 1)
    spread = jax.random.randint(key_raw, (SUBS, SUBS), 0, 1 << 20) % (ceiling + 1)
    counts = (ceiling + spread) // 2
    owner = jax.random.randint(key_full, (), 0, SUBS)
    return jnp.where(jnp.arange(SUBS)[:, None] == owner, CAP, counts).astype(jnp.int32)


def plant(entries, own_key, least, largest):
    dims = entries.shape
    index_at = [jax.random.randint(jax.random.fold_in(own_key, axis), (), 0, dims[axis]) for axis in range(len(dims))]
    entries = entries.at[tuple(index_at)].set(least)
    longest = dims.index(max(dims))
    index_at[longest] = (index_at[longest] + 1) % dims[longest]
    return entries.at[tuple(index_at)].set(largest)


def shard_levels(rng, shape, pieces, smallest, top_value):
    level, own = 1.0, jax.random.fold_in(rng, 6)
    for axis_at, shards_of in pieces:
        steps = jnp.exp(jax.random.uniform(jax.random.fold_in(own, axis_at), (shards_of,), jnp.float32, smallest / len(pieces), top_value / len(pieces)))
        level = level * jnp.repeat(steps, shape[axis_at] // shards_of).reshape([-1 if axis == axis_at else 1 for axis in range(len(shape))])
    return level


def noise(stream_key, shape, scale, bound, shards=(), dtype=jnp.bfloat16):
    array = scale * jax.random.normal(stream_key, shape, jnp.float32)
    if shards:
        array = array * shard_levels(stream_key, shape, shards, -0.22, 0.18)
    return jnp.clip(array, -bound, bound).astype(dtype)


def setup_inputs(seed: int = 0, part: int = 0) -> dict:
    key_list = jax.random.split(jax.random.key(seed), 12)
    part_splits = jax.random.split(jax.random.fold_in(key_list[11], part), 12)
    return {
        "fwd_now": noise(part_splits[0], (NI, NX, NZ), 1.0, 6.0, ((0, 2), (1, 8)), jnp.float32),
        "fwd_before": noise(part_splits[1], (NI, NX, NZ), 1.0, 6.0, ((0, 2), (1, 8)), jnp.float32),
        "adj_now": noise(part_splits[2], (NI, NX, NZ), 1.0, 6.0, ((0, 2), (1, 8)), jnp.float32),
        "adj_before": noise(part_splits[3], (NI, NX, NZ), 1.0, 6.0, ((0, 2), (1, 8)), jnp.float32),
        "velocity": jnp.clip(0.2 + 0.2 * jax.random.uniform(key_list[4], (NI, NX, NZ), jnp.float32) ** shard_levels(key_list[4], (NI, NX, NZ), ((0, 2), (1, 8)), -0.2, 0.2), 0.2, 0.4),
        "log_density": jnp.clip(jax.random.uniform(key_list[5], (NI, NX, NZ), jnp.float32, -0.3, 0.3) * shard_levels(key_list[5], (NI, NX, NZ), ((0, 2), (1, 8)), -0.4, 0.0), -0.3, 0.3),
        "observed": noise(part_splits[6], (NT, SUBS * SUBS * CAP), 8.0, 48.0, ((1, 16),), jnp.float32),
        "rec_cells": plant(jax.random.randint(key_list[7], (SUBS, SUBS * CAP), 0, CI * CX * NZ), jax.random.fold_in(key_list[7], 1), 0, (CI * CX * NZ) - 1).astype(jnp.int32),
        "rec_counts": draw_rec_counts(jax.random.fold_in(key_list[11], 71), part),
        "src_cell": plant(jax.random.randint(part_splits[9], (NSRC,), 0, NI * NX * NZ), jax.random.fold_in(part_splits[9], 1), 0, (NI * NX * NZ) - 1).astype(jnp.int32),
        "wavelet": noise(part_splits[10], (NT, NSRC), 24.0, 144.0, (), jnp.float32),
    }


SECOND_COEFFS = (-205.0 / 72.0, 8.0 / 5.0, -1.0 / 5.0, 8.0 / 315.0, -1.0 / 560.0)
FIRST_COEFFS = (4.0 / 5.0, -1.0 / 5.0, 4.0 / 105.0, -1.0 / 280.0)


def differences(padded):
    inner_a = padded.shape[0] - 8
    inner_b = padded.shape[1] - 8
    center = padded[4:4 + inner_a, 4:4 + inner_b]
    extent = center.shape[2]
    deep_pad = jnp.pad(center, ((0, 0), (0, 0), (4, 4)))
    laplace = (3.0 * SECOND_COEFFS[0]) * center
    slope_i = jnp.zeros_like(center)
    slope_x = jnp.zeros_like(center)
    slope_z = jnp.zeros_like(center)
    for offset in range(1, 5):
        plus_i = padded[4 + offset:4 + offset + inner_a, 4:4 + inner_b]
        minus_i = padded[4 - offset:4 - offset + inner_a, 4:4 + inner_b]
        plus_x = padded[4:4 + inner_a, 4 + offset:4 + offset + inner_b]
        minus_x = padded[4:4 + inner_a, 4 - offset:4 - offset + inner_b]
        plus_z = deep_pad[:, :, 4 + offset:4 + offset + extent]
        minus_z = deep_pad[:, :, 4 - offset:4 - offset + extent]
        weight_first = FIRST_COEFFS[offset - 1]
        slope_i = slope_i + weight_first * (plus_i - minus_i)
        slope_x = slope_x + weight_first * (plus_x - minus_x)
        slope_z = slope_z + weight_first * (plus_z - minus_z)
        laplace = laplace + SECOND_COEFFS[offset] * (plus_i + minus_i + plus_x + minus_x + plus_z + minus_z)
    return laplace, (slope_i, slope_x, slope_z)


def wave_operator(padded, density_slopes, speed_sq):
    laplace, slopes = differences(padded)
    coupling = density_slopes[0] * slopes[0] + density_slopes[1] * slopes[1] + density_slopes[2] * slopes[2]
    return speed_sq * (laplace - coupling)


def pad_four(values):
    return jnp.pad(values, ((4, 4), (4, 4), (0, 0)))


def reference(fwd_now, fwd_before, adj_now, adj_before, velocity, log_density, observed, rec_cells, rec_counts, src_cell, wavelet):
    cell_total = NI * NX * NZ
    spare_term, density_slopes = differences(pad_four(log_density))
    speed_sq = velocity * velocity
    history = [fwd_before, fwd_now]
    for moment in range(NT):
        current = history[-1]
        source_field = jnp.zeros((cell_total,), jnp.float32).at[src_cell].add(wavelet[moment]).reshape(NI, NX, NZ)
        history.append(2.0 * current - history[-2] + wave_operator(pad_four(current), density_slopes, speed_sq) + source_field)
    owner_ids = jnp.arange(SUBS).astype(jnp.int32)
    owner_x = owner_ids // N_INLINE
    owner_i = owner_ids % N_INLINE
    local_i = rec_cells // (CX * NZ)
    local_x = (rec_cells // NZ) % CX
    local_z = rec_cells % NZ
    global_cell = ((owner_i[:, None] * CI + local_i) * NX + owner_x[:, None] * CX + local_x) * NZ + local_z
    live_mask = (jnp.arange(CAP).astype(jnp.int32)[None, None, :] < rec_counts[:, :, None]).astype(jnp.float32).reshape(SUBS, SUBS * CAP)
    routed = observed.reshape(NT, SUBS, SUBS, CAP).transpose(0, 2, 1, 3).reshape(NT, SUBS, SUBS * CAP)
    predicted = jnp.stack([history[moment + 2].reshape(-1)[global_cell] for moment in range(NT)])
    residual = live_mask[None] * (predicted - routed)
    flat_cells = global_cell.reshape(-1)
    adjoint = [adj_before, adj_now]
    image_sum = jnp.zeros_like(fwd_now)
    for back_step in range(NT):
        moment = NT - 1 - back_step
        current = adjoint[-1]
        injected = jnp.zeros((cell_total,), jnp.float32).at[flat_cells].add(residual[moment].reshape(-1)).reshape(NI, NX, NZ)
        fresh_state = 2.0 * current - adjoint[-2] + wave_operator(pad_four(current), density_slopes, speed_sq) + injected
        adjoint.append(fresh_state)
        image_sum = image_sum + fresh_state * (history[moment + 2] - 2.0 * history[moment + 1] + history[moment])
    raw_gradient = image_sum * (2.0 / NT) / velocity
    positions = jnp.arange(NX).astype(jnp.float32)
    kernel = jnp.exp(-jnp.abs(positions[:, None] - positions[None, :]) / SMOOTH)
    kernel = kernel / jnp.sum(kernel, axis=1, keepdims=True)
    gradient = jnp.einsum("ixz,yx->ziy", raw_gradient, kernel, precision=lax.Precision.HIGHEST)
    return gradient, adjoint[-1], adjoint[-2]
```

```python
import functools

import jax
import jax.numpy as jnp
from jax import lax
from jax.experimental import pallas as pl
from jax.experimental.pallas import tpu as pltpu
from jax.sharding import PartitionSpec as P

CAP = 8
SMOOTH = 16
MESH = pl.DeviceIdType.MESH

SECOND_COEFFS = (-205.0 / 72.0, 8.0 / 5.0, -1.0 / 5.0, 8.0 / 315.0, -1.0 / 560.0)
FIRST_COEFFS = (4.0 / 5.0, -1.0 / 5.0, 4.0 / 105.0, -1.0 / 280.0)
LEFT, RIGHT, UP, DOWN = 0, 1, 2, 3
DENSITY = 4


def split_bf16(value):
    high = value.astype(jnp.bfloat16)
    low = (value - high.astype(jnp.float32)).astype(jnp.bfloat16)
    return high, low


def dot(a, b):
    return jnp.dot(a, b, preferred_element_type=jnp.float32)


def wave_kernel(
    sizes,
    fwd_now, fwd_before, adj_now, adj_before, velocity, density,
    traces, rec_row, rec_row_t, rec_z, rec_live, src_row, src_z, wavelet,
    raw_out, last_out, previous_out,
    field, x_in, x_out, accel, base, image, slopes, speed_sq,
    row_map, row_map_t, z_map, z_high, z_low, residual_ref,
    send_sem, recv_sem,
):
    n_i, n_x, depth, steps, n_xline, n_inline = sizes
    rows = n_i * n_x
    xl = lax.axis_index("xline")
    core = lax.axis_index("inline")
    side = lax.rem(xl, 2)
    half = lax.rem(side + lax.rem(core, 2), 2)
    mate = xl + 1 - 2 * side
    has = (
        xl >= 2,
        xl < n_xline - 2,
        core * 2 + half > 0,
        core * 2 + half < 2 * n_inline - 1,
    )
    target = (
        {"xline": xl - 2},
        {"xline": xl + 2},
        {"xline": jnp.where(half == 1, mate, xl), "inline": jnp.where(half == 1, core, core - 1)},
        {"xline": jnp.where(half == 0, mate, xl), "inline": jnp.where(half == 0, core, core + 1)},
    )
    inner_x = pl.ds(8, n_x)

    def copy_of(idx, way):
        if way == LEFT:
            src, dst = x_out.at[idx, 0], x_in.at[idx, 1]
        elif way == RIGHT:
            src, dst = x_out.at[idx, 1], x_in.at[idx, 0]
        elif way == UP:
            src = field.at[idx, pl.ds(4, 4), inner_x, :]
            dst = field.at[idx, pl.ds(n_i + 4, 4), inner_x, :]
        else:
            src = field.at[idx, pl.ds(n_i, 4), inner_x, :]
            dst = field.at[idx, pl.ds(0, 4), inner_x, :]
        return pltpu.make_async_remote_copy(
            src_ref=src, dst_ref=dst,
            send_sem=send_sem.at[idx, way], recv_sem=recv_sem.at[idx, way],
            device_id=target[way], device_id_type=MESH,
        )

    def send(idx):
        x_out[idx, 0] = field[idx, pl.ds(4, n_i), pl.ds(8, 4), :]
        x_out[idx, 1] = field[idx, pl.ds(4, n_i), pl.ds(4 + n_x, 4), :]
        for way in range(4):
            @pl.when(has[way])
            def _():
                copy_of(idx, way).start()

    def finish(idx):
        for way in range(4):
            @pl.when(has[way])
            def _():
                copy_of(idx, way).wait_send()
                copy_of(idx, way ^ 1).wait_recv()
        field[idx, pl.ds(4, n_i), pl.ds(4, 4), :] = x_in[idx, 0]
        field[idx, pl.ds(4, n_i), pl.ds(8 + n_x, 4), :] = x_in[idx, 1]

    for idx in range(5):
        field[idx, pl.ds(0, 4)] = jnp.zeros((4,) + field.shape[2:], jnp.float32)
        field[idx, pl.ds(n_i + 4, 4)] = jnp.zeros((4,) + field.shape[2:], jnp.float32)
    x_in[...] = jnp.zeros(x_in.shape, jnp.float32)

    barrier = pltpu.get_barrier_semaphore()
    for way in range(4):
        @pl.when(has[way])
        def _():
            pl.semaphore_signal(barrier, inc=1, device_id=target[way], device_id_type=MESH)
    pl.semaphore_wait(barrier, sum(present.astype(jnp.int32) for present in has))

    inner_i = pl.ds(4, n_i)
    field[DENSITY, inner_i, inner_x, :] = density[...]
    field[0, inner_i, inner_x, :] = fwd_now[...]
    send(DENSITY)
    send(0)
    field[2, inner_i, inner_x, :] = adj_now[...]
    send(2)
    field[1, inner_i, inner_x, :] = fwd_before[...]
    field[3, inner_i, inner_x, :] = adj_before[...]

    speed_sq[...] = velocity[...] * velocity[...]
    image[...] = jnp.zeros(image.shape, jnp.float32)
    slots = rec_row.shape[0]
    row_map[...] = (lax.broadcasted_iota(jnp.int32, (rows, slots), 0) == rec_row_t[...]).astype(jnp.float32).astype(jnp.bfloat16)
    row_map_t[...] = (lax.broadcasted_iota(jnp.int32, (slots, rows), 1) == rec_row[...]).astype(jnp.float32).astype(jnp.bfloat16)
    z_map[...] = (lax.broadcasted_iota(jnp.int32, (slots, depth), 1) == rec_z[...]).astype(jnp.float32)
    src_rows = (lax.broadcasted_iota(jnp.int32, (rows, src_row.shape[1]), 0) == src_row[...]).astype(jnp.float32)
    src_cols = (lax.broadcasted_iota(jnp.int32, (src_z.shape[0], depth), 1) == src_z[...]).astype(jnp.float32).astype(jnp.bfloat16)
    offset = lax.broadcasted_iota(jnp.int32, (depth, depth), 0) - lax.broadcasted_iota(jnp.int32, (depth, depth), 1)
    second = jnp.where(offset == 0, 3.0 * SECOND_COEFFS[0], 0.0)
    first = jnp.zeros((depth, depth), jnp.float32)
    for k in range(1, 5):
        second = jnp.where((offset == k) | (offset == -k), SECOND_COEFFS[k], second)
        first = jnp.where(offset == k, FIRST_COEFFS[k - 1], first)
        first = jnp.where(offset == -k, -FIRST_COEFFS[k - 1], first)
    high, low = split_bf16(second)
    z_high[:, pl.ds(0, depth)] = high
    z_low[:, pl.ds(0, depth)] = low
    high, low = split_bf16(first)
    z_high[:, pl.ds(depth, depth)] = high
    z_low[:, pl.ds(depth, depth)] = low

    def flat(idx):
        return field[idx, inner_i, inner_x, :].reshape(rows, depth)

    def along_depth(idx):
        high, low = split_bf16(flat(idx))
        both = dot(high, z_high[...]) + (dot(low, z_high[...]) + dot(high, z_low[...]))
        return both[:, :depth], both[:, depth:]

    def across(idx, i):
        lap = slope_i = slope_x = None
        for k in range(1, 5):
            plus_i = field[idx, i + 4 + k, inner_x, :]
            minus_i = field[idx, i + 4 - k, inner_x, :]
            plus_x = field[idx, i + 4, pl.ds(8 + k, n_x), :]
            minus_x = field[idx, i + 4, pl.ds(8 - k, n_x), :]
            terms = (
                SECOND_COEFFS[k] * ((plus_i + minus_i) + (plus_x + minus_x)),
                FIRST_COEFFS[k - 1] * (plus_i - minus_i),
                FIRST_COEFFS[k - 1] * (plus_x - minus_x),
            )
            if lap is None:
                lap, slope_i, slope_x = terms
            else:
                lap, slope_i, slope_x = lap + terms[0], slope_i + terms[1], slope_x + terms[2]
        return lap, slope_i, slope_x

    def prepare(idx, term):
        lap, slope = along_depth(idx)
        partial = term + speed_sq[...].reshape(rows, depth) * (lap - slopes[2].reshape(rows, depth) * slope)
        base[...] = partial.reshape(n_i, n_x, depth)

    slopes[2] = along_depth(DENSITY)[1].reshape(n_i, n_x, depth)
    finish(DENSITY)

    @pl.loop(0, n_i)
    def _(i):
        _, slope_i, slope_x = across(DENSITY, i)
        slopes[0, i] = slope_i
        slopes[1, i] = slope_x

    @pl.loop(0, steps)
    def _(t):
        now = lax.rem(t, 2)
        other = 1 - now
        high, low = split_bf16(src_rows * wavelet[pl.ds(t, 1), :])
        prepare(now, dot(high, src_cols) + dot(low, src_cols))
        finish(now)

        @pl.loop(0, n_i)
        def _(i):
            lap, slope_i, slope_x = across(now, i)
            change = base[i] + speed_sq[i] * (lap - slopes[0, i] * slope_i - slopes[1, i] * slope_x)
            accel[t, i] = change
            field[other, i + 4, inner_x, :] = (
                2.0 * field[now, i + 4, inner_x, :] - field[other, i + 4, inner_x, :] + change
            )

        @pl.when(t < steps - 1)
        def _():
            send(other)

        high, low = split_bf16(flat(other))
        picked = dot(row_map_t[...], high) + dot(row_map_t[...], low)
        predicted = jnp.sum(picked * z_map[...], axis=1, keepdims=True)
        column = lax.broadcasted_iota(jnp.int32, traces.shape, 1) == t
        seen = jnp.sum(jnp.where(column, traces[...], 0.0), axis=1, keepdims=True)
        residual_ref[t] = rec_live[...] * (predicted - seen)

    @pl.loop(0, steps)
    def _(j):
        now = 2 + lax.rem(j, 2)
        other = 5 - now
        t = steps - 1 - j
        high, low = split_bf16(residual_ref[t] * z_map[...])
        prepare(now, dot(row_map[...], high) + dot(row_map[...], low))
        finish(now)

        @pl.loop(0, n_i)
        def _(i):
            lap, slope_i, slope_x = across(now, i)
            change = base[i] + speed_sq[i] * (lap - slopes[0, i] * slope_i - slopes[1, i] * slope_x)
            fresh = 2.0 * field[now, i + 4, inner_x, :] - field[other, i + 4, inner_x, :] + change
            field[other, i + 4, inner_x, :] = fresh
            image[i] += fresh * accel[t, i]

        @pl.when(j < steps - 1)
        def _():
            send(other)

    raw_out[...] = image[...] * (2.0 / steps) / velocity[...]
    last_out[...] = field[2 + steps % 2, inner_i, inner_x, :]
    previous_out[...] = field[2 + (steps - 1) % 2, inner_i, inner_x, :]


def per_device(
    fwd_now, fwd_before, adj_now, adj_before, velocity, log_density,
    observed, rec_cells, rec_counts, src_cell, wavelet,
):
    tile_i, tile_x, depth = fwd_now.shape
    steps = wavelet.shape[0]
    n_xline = lax.axis_size("xline")
    n_inline = lax.axis_size("inline")
    full_x = tile_x * n_xline
    n_i, n_x = tile_i // 2, tile_x * 2
    xl = lax.axis_index("xline")
    core = lax.axis_index("inline")
    side = xl % 2
    half = (side + core) % 2
    swap = [(k, k ^ 1) for k in range(n_xline)]

    def pair_up(mine, theirs, axis):
        return jnp.where(
            side == 0,
            jnp.concatenate([mine, theirs], axis=axis),
            jnp.concatenate([theirs, mine], axis=axis),
        )

    def gather_pair(value):
        kept = lax.dynamic_slice_in_dim(value, half * n_i, n_i, axis=0)
        sent = lax.dynamic_slice_in_dim(value, (1 - half) * n_i, n_i, axis=0)
        return pair_up(kept, lax.ppermute(sent, "xline", swap), 1)

    routed = lax.all_to_all(observed, ("xline", "inline"), split_axis=1, concat_axis=1, tiled=True)
    live = (jnp.arange(CAP)[None, :] < rec_counts[0][:, None]).astype(jnp.int32).reshape(1, -1)
    lists = jnp.concatenate([rec_cells, live], axis=0)
    lists = pair_up(lists, lax.ppermute(lists, "xline", swap), 1)
    traces = pair_up(routed, lax.ppermute(routed, "xline", swap), 1).T
    cells = lists[0]
    slots = cells.shape[0]
    cell_i = cells // (tile_x * depth) - half * n_i
    cell_x = cells // depth % tile_x + jnp.where(jnp.arange(slots) < slots // 2, 0, tile_x)
    rec_row = jnp.where((cell_i >= 0) & (cell_i < n_i), cell_i * n_x + cell_x, -1)
    rec_z = cells % depth
    src_i = src_cell // (full_x * depth) - (core * tile_i + half * n_i)
    src_x = src_cell // depth % full_x - (xl // 2) * n_x
    inside = (src_i >= 0) & (src_i < n_i) & (src_x >= 0) & (src_x < n_x)
    src_row = jnp.where(inside, src_i * n_x + src_x, -1)
    src_z = src_cell % depth

    block = (n_i, n_x, depth)
    rows = n_i * n_x
    vmem = pl.BlockSpec(memory_space=pltpu.VMEM)
    kernel = functools.partial(wave_kernel, (n_i, n_x, depth, steps, n_xline, n_inline))
    raw, last, previous = pl.pallas_call(
        kernel,
        out_shape=[jax.ShapeDtypeStruct(block, jnp.float32)] * 3,
        in_specs=[vmem] * 14,
        out_specs=[vmem] * 3,
        scratch_shapes=[
            pltpu.VMEM((5, n_i + 8, n_x + 16, depth), jnp.float32),
            pltpu.VMEM((5, 2, n_i, 4, depth), jnp.float32),
            pltpu.VMEM((5, 2, n_i, 4, depth), jnp.float32),
            pltpu.VMEM((steps,) + block, jnp.float32),
            pltpu.VMEM(block, jnp.float32),
            pltpu.VMEM(block, jnp.float32),
            pltpu.VMEM((3,) + block, jnp.float32),
            pltpu.VMEM(block, jnp.float32),
            pltpu.VMEM((rows, slots), jnp.bfloat16),
            pltpu.VMEM((slots, rows), jnp.bfloat16),
            pltpu.VMEM((slots, depth), jnp.float32),
            pltpu.VMEM((depth, 2 * depth), jnp.bfloat16),
            pltpu.VMEM((depth, 2 * depth), jnp.bfloat16),
            pltpu.VMEM((steps, slots, 1), jnp.float32),
            pltpu.SemaphoreType.DMA((5, 4)),
            pltpu.SemaphoreType.DMA((5, 4)),
        ],
        compiler_params=pltpu.CompilerParams(
            collective_id=0, has_side_effects=True, vmem_limit_bytes=56 * 1024 * 1024
        ),
    )(
        gather_pair(fwd_now), gather_pair(fwd_before), gather_pair(adj_now), gather_pair(adj_before),
        gather_pair(velocity), gather_pair(log_density),
        traces, rec_row[:, None], rec_row[None, :], rec_z[:, None],
        lists[1].astype(jnp.float32)[:, None], src_row[None, :], src_z[:, None], wavelet,
    )

    def split_pair(value):
        kept = lax.dynamic_slice_in_dim(value, side * tile_x, tile_x, axis=1)
        sent = lax.dynamic_slice_in_dim(value, (1 - side) * tile_x, tile_x, axis=1)
        got = lax.ppermute(sent, "xline", swap)
        return jnp.where(
            half == 0, jnp.concatenate([kept, got], axis=0), jnp.concatenate([got, kept], axis=0)
        )

    pieces = n_xline
    columns = lax.all_to_all(
        raw.reshape(n_i, n_x, pieces, depth // pieces).transpose(2, 0, 1, 3),
        "xline", split_axis=0, concat_axis=0, tiled=True,
    ).reshape(n_xline // 2, 2, n_i, n_x, depth // pieces)
    columns = jnp.where(core % 2 == 0, columns, columns[:, ::-1])
    positions = jnp.arange(full_x).astype(jnp.float32)
    weights = jnp.exp(-jnp.abs(positions[:, None] - positions[None, :]) / SMOOTH)
    weights = weights / jnp.sum(weights, axis=1, keepdims=True)
    gradient = jnp.einsum(
        "phixz,ypx->zhiy", columns, weights.reshape(full_x, n_xline // 2, n_x),
        precision=lax.Precision.HIGHEST,
    ).reshape(depth // pieces, tile_i, full_x)
    return gradient, split_pair(last), split_pair(previous)


def solution(mesh):
    return jax.shard_map(
        per_device,
        mesh=mesh,
        in_specs=(
            P(("shots", "inline"), "xline", None),
            P(("shots", "inline"), "xline", None),
            P(("shots", "inline"), "xline", None),
            P(("shots", "inline"), "xline", None),
            P("inline", "xline", None),
            P("inline", "xline", None),
            P("shots", ("xline", "inline")),
            P(("xline", "inline"), None),
            P(("xline", "inline"), None),
            P("shots"),
            P("shots", None),
        ),
        out_specs=(
            P(("shots", "xline"), "inline", None),
            P(("shots", "inline"), "xline", None),
            P(("shots", "inline"), "xline", None),
        ),
        check_vma=False,
    )
```

```python
import functools

import jax
import jax.numpy as jnp
from jax import lax
from jax.experimental import pallas as pl
from jax.experimental.pallas import tpu as pltpu
from jax.sharding import PartitionSpec as P

CAP = 8
SMOOTH = 16
MESH = pl.DeviceIdType.MESH

SECOND_COEFFS = (-205.0 / 72.0, 8.0 / 5.0, -1.0 / 5.0, 8.0 / 315.0, -1.0 / 560.0)
FIRST_COEFFS = (4.0 / 5.0, -1.0 / 5.0, 4.0 / 105.0, -1.0 / 280.0)
LEFT, RIGHT, UP, DOWN = 0, 1, 2, 3
DENSITY = 4


def split_bf16(value):
    high = value.astype(jnp.bfloat16)
    low = (value - high.astype(jnp.float32)).astype(jnp.bfloat16)
    return high, low


def dot(a, b):
    return jnp.dot(a, b, preferred_element_type=jnp.float32)


def wave_kernel(
    sizes,
    fwd_now, fwd_before, adj_now, adj_before, velocity, density,
    traces, rec_row, rec_row_t, rec_z, rec_live, src_row, src_z, wavelet,
    raw_out, last_out, previous_out,
    field, x_in, x_out, accel, base, image, slopes, speed_sq,
    row_map, row_map_t, z_map, z_high, z_low, residual_ref,
    send_sem, recv_sem,
):
    n_i, n_x, depth, steps, n_xline, n_inline = sizes
    rows = n_i * n_x
    xl = lax.axis_index("xline")
    core = lax.axis_index("inline")
    side = lax.rem(xl, 2)
    half = lax.rem(side + lax.rem(core, 2), 2)
    mate = xl + 1 - 2 * side
    has = (
        xl >= 2,
        xl < n_xline - 2,
        core * 2 + half > 0,
        core * 2 + half < 2 * n_inline - 1,
    )
    target = (
        {"xline": xl - 2},
        {"xline": xl + 2},
        {"xline": jnp.where(half == 1, mate, xl), "inline": jnp.where(half == 1, core, core - 1)},
        {"xline": jnp.where(half == 0, mate, xl), "inline": jnp.where(half == 0, core, core + 1)},
    )
    inner_x = pl.ds(8, n_x)

    middle = n_i // 2

    def copy_of(idx, way, part):
        part_rows = pl.ds(part * middle, middle)
        sem = way
        if way == LEFT:
            src, dst = x_out.at[idx, 0, part_rows], x_in.at[idx, 1, part_rows]
            sem = way + 4 * part
        elif way == RIGHT:
            src, dst = x_out.at[idx, 1, part_rows], x_in.at[idx, 0, part_rows]
            sem = way + 4 * part
        elif way == UP:
            src = field.at[idx, pl.ds(4, 4), inner_x, :]
            dst = field.at[idx, pl.ds(n_i + 4, 4), inner_x, :]
        else:
            src = field.at[idx, pl.ds(n_i, 4), inner_x, :]
            dst = field.at[idx, pl.ds(0, 4), inner_x, :]
        return pltpu.make_async_remote_copy(
            src_ref=src, dst_ref=dst,
            send_sem=send_sem.at[idx, sem], recv_sem=recv_sem.at[idx, sem],
            device_id=target[way], device_id_type=MESH,
        )

    def send(idx, part):
        part_rows = pl.ds(part * middle, middle)
        field_rows = pl.ds(4 + part * middle, middle)
        x_out[idx, 0, part_rows] = field[idx, field_rows, pl.ds(8, 4), :]
        x_out[idx, 1, part_rows] = field[idx, field_rows, pl.ds(4 + n_x, 4), :]
        for way in (LEFT, RIGHT, UP + part):
            @pl.when(has[way])
            def _():
                copy_of(idx, way, part).start()

    def finish(idx, part):
        for way in (LEFT, RIGHT, UP + part):
            @pl.when(has[way])
            def _():
                copy_of(idx, way, part).wait_send()
                copy_of(idx, way ^ 1, part).wait_recv()
        part_rows = pl.ds(part * middle, middle)
        field_rows = pl.ds(4 + part * middle, middle)
        field[idx, field_rows, pl.ds(4, 4), :] = x_in[idx, 0, part_rows]
        field[idx, field_rows, pl.ds(8 + n_x, 4), :] = x_in[idx, 1, part_rows]

    for idx in range(5):
        field[idx, pl.ds(0, 4)] = jnp.zeros((4,) + field.shape[2:], jnp.float32)
        field[idx, pl.ds(n_i + 4, 4)] = jnp.zeros((4,) + field.shape[2:], jnp.float32)
    x_in[...] = jnp.zeros(x_in.shape, jnp.float32)

    barrier = pltpu.get_barrier_semaphore()
    for way in range(4):
        @pl.when(has[way])
        def _():
            pl.semaphore_signal(barrier, inc=1, device_id=target[way], device_id_type=MESH)
    pl.semaphore_wait(barrier, sum(present.astype(jnp.int32) for present in has))

    inner_i = pl.ds(4, n_i)
    field[DENSITY, inner_i, inner_x, :] = density[...]
    field[0, inner_i, inner_x, :] = fwd_now[...]
    send(DENSITY, 0)
    send(DENSITY, 1)
    send(0, 0)
    send(0, 1)
    field[2, inner_i, inner_x, :] = adj_now[...]
    send(2, 0)
    send(2, 1)
    field[1, inner_i, inner_x, :] = fwd_before[...]
    field[3, inner_i, inner_x, :] = adj_before[...]

    speed_sq[...] = velocity[...] * velocity[...]
    image[...] = jnp.zeros(image.shape, jnp.float32)
    slots = rec_row.shape[0]
    row_map[...] = (lax.broadcasted_iota(jnp.int32, (rows, slots), 0) == rec_row_t[...]).astype(jnp.float32).astype(jnp.bfloat16)
    row_map_t[...] = (lax.broadcasted_iota(jnp.int32, (slots, rows), 1) == rec_row[...]).astype(jnp.float32).astype(jnp.bfloat16)
    z_map[...] = (lax.broadcasted_iota(jnp.int32, (slots, depth), 1) == rec_z[...]).astype(jnp.float32)
    src_rows = (lax.broadcasted_iota(jnp.int32, (rows, src_row.shape[1]), 0) == src_row[...]).astype(jnp.float32)
    src_cols = (lax.broadcasted_iota(jnp.int32, (src_z.shape[0], depth), 1) == src_z[...]).astype(jnp.float32).astype(jnp.bfloat16)
    offset = lax.broadcasted_iota(jnp.int32, (depth, depth), 0) - lax.broadcasted_iota(jnp.int32, (depth, depth), 1)
    second = jnp.where(offset == 0, 3.0 * SECOND_COEFFS[0], 0.0)
    first = jnp.zeros((depth, depth), jnp.float32)
    for k in range(1, 5):
        second = jnp.where((offset == k) | (offset == -k), SECOND_COEFFS[k], second)
        first = jnp.where(offset == k, FIRST_COEFFS[k - 1], first)
        first = jnp.where(offset == -k, -FIRST_COEFFS[k - 1], first)
    high, low = split_bf16(second)
    z_high[:, pl.ds(0, depth)] = high
    z_low[:, pl.ds(0, depth)] = low
    high, low = split_bf16(first)
    z_high[:, pl.ds(depth, depth)] = high
    z_low[:, pl.ds(depth, depth)] = low

    def flat(idx):
        return field[idx, inner_i, inner_x, :].reshape(rows, depth)

    def along_depth(idx):
        high, low = split_bf16(flat(idx))
        both = dot(high, z_high[...]) + (dot(low, z_high[...]) + dot(high, z_low[...]))
        return both[:, :depth], both[:, depth:]

    def across(idx, i):
        lap = slope_i = slope_x = None
        for k in range(1, 5):
            plus_i = field[idx, i + 4 + k, inner_x, :]
            minus_i = field[idx, i + 4 - k, inner_x, :]
            plus_x = field[idx, i + 4, pl.ds(8 + k, n_x), :]
            minus_x = field[idx, i + 4, pl.ds(8 - k, n_x), :]
            terms = (
                SECOND_COEFFS[k] * ((plus_i + minus_i) + (plus_x + minus_x)),
                FIRST_COEFFS[k - 1] * (plus_i - minus_i),
                FIRST_COEFFS[k - 1] * (plus_x - minus_x),
            )
            if lap is None:
                lap, slope_i, slope_x = terms
            else:
                lap, slope_i, slope_x = lap + terms[0], slope_i + terms[1], slope_x + terms[2]
        return lap, slope_i, slope_x

    def prepare(idx, term):
        lap, slope = along_depth(idx)
        partial = term + speed_sq[...].reshape(rows, depth) * (lap - slopes[2].reshape(rows, depth) * slope)
        base[...] = partial.reshape(n_i, n_x, depth)

    slopes[2] = along_depth(DENSITY)[1].reshape(n_i, n_x, depth)
    finish(DENSITY, 0)
    finish(DENSITY, 1)

    @pl.loop(0, n_i)
    def _(i):
        _, slope_i, slope_x = across(DENSITY, i)
        slopes[0, i] = slope_i
        slopes[1, i] = slope_x

    @pl.loop(0, steps)
    def _(t):
        now = lax.rem(t, 2)
        other = 1 - now
        high, low = split_bf16(src_rows * wavelet[pl.ds(t, 1), :])
        prepare(now, dot(high, src_cols) + dot(low, src_cols))

        for part in range(2):
            finish(now, part)

            @pl.loop(part * middle, (part + 1) * middle)
            def _(i):
                lap, slope_i, slope_x = across(now, i)
                change = base[i] + speed_sq[i] * (lap - slopes[0, i] * slope_i - slopes[1, i] * slope_x)
                accel[t, i] = change
                field[other, i + 4, inner_x, :] = (
                    2.0 * field[now, i + 4, inner_x, :] - field[other, i + 4, inner_x, :] + change
                )

            @pl.when(t < steps - 1)
            def _():
                send(other, part)

        high, low = split_bf16(flat(other))
        picked = dot(row_map_t[...], high) + dot(row_map_t[...], low)
        predicted = jnp.sum(picked * z_map[...], axis=1, keepdims=True)
        column = lax.broadcasted_iota(jnp.int32, traces.shape, 1) == t
        seen = jnp.sum(jnp.where(column, traces[...], 0.0), axis=1, keepdims=True)
        residual_ref[t] = rec_live[...] * (predicted - seen)

    @pl.loop(0, steps)
    def _(j):
        now = 2 + lax.rem(j, 2)
        other = 5 - now
        t = steps - 1 - j
        high, low = split_bf16(residual_ref[t] * z_map[...])
        prepare(now, dot(row_map[...], high) + dot(row_map[...], low))

        for part in range(2):
            finish(now, part)

            @pl.loop(part * middle, (part + 1) * middle)
            def _(i):
                lap, slope_i, slope_x = across(now, i)
                change = base[i] + speed_sq[i] * (lap - slopes[0, i] * slope_i - slopes[1, i] * slope_x)
                fresh = 2.0 * field[now, i + 4, inner_x, :] - field[other, i + 4, inner_x, :] + change
                field[other, i + 4, inner_x, :] = fresh
                image[i] += fresh * accel[t, i]

            @pl.when(j < steps - 1)
            def _():
                send(other, part)

    raw_out[...] = image[...] * (2.0 / steps) / velocity[...]
    last_out[...] = field[2 + steps % 2, inner_i, inner_x, :]
    previous_out[...] = field[2 + (steps - 1) % 2, inner_i, inner_x, :]


def per_device(
    fwd_now, fwd_before, adj_now, adj_before, velocity, log_density,
    observed, rec_cells, rec_counts, src_cell, wavelet,
):
    tile_i, tile_x, depth = fwd_now.shape
    steps = wavelet.shape[0]
    n_xline = lax.axis_size("xline")
    n_inline = lax.axis_size("inline")
    full_x = tile_x * n_xline
    n_i, n_x = tile_i // 2, tile_x * 2
    xl = lax.axis_index("xline")
    core = lax.axis_index("inline")
    side = xl % 2
    half = (side + core) % 2
    swap = [(k, k ^ 1) for k in range(n_xline)]

    def pair_up(mine, theirs, axis):
        return jnp.where(
            side == 0,
            jnp.concatenate([mine, theirs], axis=axis),
            jnp.concatenate([theirs, mine], axis=axis),
        )

    def gather_pair(value):
        kept = lax.dynamic_slice_in_dim(value, half * n_i, n_i, axis=0)
        sent = lax.dynamic_slice_in_dim(value, (1 - half) * n_i, n_i, axis=0)
        return pair_up(kept, lax.ppermute(sent, "xline", swap), 1)

    routed = lax.all_to_all(observed, ("xline", "inline"), split_axis=1, concat_axis=1, tiled=True)
    live = (jnp.arange(CAP)[None, :] < rec_counts[0][:, None]).astype(jnp.int32).reshape(1, -1)
    lists = jnp.concatenate([rec_cells, live], axis=0)
    lists = pair_up(lists, lax.ppermute(lists, "xline", swap), 1)
    traces = pair_up(routed, lax.ppermute(routed, "xline", swap), 1).T
    cells = lists[0]
    slots = cells.shape[0]
    cell_i = cells // (tile_x * depth) - half * n_i
    cell_x = cells // depth % tile_x + jnp.where(jnp.arange(slots) < slots // 2, 0, tile_x)
    rec_row = jnp.where((cell_i >= 0) & (cell_i < n_i), cell_i * n_x + cell_x, -1)
    rec_z = cells % depth
    src_i = src_cell // (full_x * depth) - (core * tile_i + half * n_i)
    src_x = src_cell // depth % full_x - (xl // 2) * n_x
    inside = (src_i >= 0) & (src_i < n_i) & (src_x >= 0) & (src_x < n_x)
    src_row = jnp.where(inside, src_i * n_x + src_x, -1)
    src_z = src_cell % depth

    block = (n_i, n_x, depth)
    rows = n_i * n_x
    vmem = pl.BlockSpec(memory_space=pltpu.VMEM)
    kernel = functools.partial(wave_kernel, (n_i, n_x, depth, steps, n_xline, n_inline))
    raw, last, previous = pl.pallas_call(
        kernel,
        out_shape=[jax.ShapeDtypeStruct(block, jnp.float32)] * 3,
        in_specs=[vmem] * 14,
        out_specs=[vmem] * 3,
        scratch_shapes=[
            pltpu.VMEM((5, n_i + 8, n_x + 16, depth), jnp.float32),
            pltpu.VMEM((5, 2, n_i, 4, depth), jnp.float32),
            pltpu.VMEM((5, 2, n_i, 4, depth), jnp.float32),
            pltpu.VMEM((steps,) + block, jnp.float32),
            pltpu.VMEM(block, jnp.float32),
            pltpu.VMEM(block, jnp.float32),
            pltpu.VMEM((3,) + block, jnp.float32),
            pltpu.VMEM(block, jnp.float32),
            pltpu.VMEM((rows, slots), jnp.bfloat16),
            pltpu.VMEM((slots, rows), jnp.bfloat16),
            pltpu.VMEM((slots, depth), jnp.float32),
            pltpu.VMEM((depth, 2 * depth), jnp.bfloat16),
            pltpu.VMEM((depth, 2 * depth), jnp.bfloat16),
            pltpu.VMEM((steps, slots, 1), jnp.float32),
            pltpu.SemaphoreType.DMA((5, 6)),
            pltpu.SemaphoreType.DMA((5, 6)),
        ],
        compiler_params=pltpu.CompilerParams(
            collective_id=0, has_side_effects=True, vmem_limit_bytes=56 * 1024 * 1024
        ),
    )(
        gather_pair(fwd_now), gather_pair(fwd_before), gather_pair(adj_now), gather_pair(adj_before),
        gather_pair(velocity), gather_pair(log_density),
        traces, rec_row[:, None], rec_row[None, :], rec_z[:, None],
        lists[1].astype(jnp.float32)[:, None], src_row[None, :], src_z[:, None], wavelet,
    )

    def split_pair(value):
        kept = lax.dynamic_slice_in_dim(value, side * tile_x, tile_x, axis=1)
        sent = lax.dynamic_slice_in_dim(value, (1 - side) * tile_x, tile_x, axis=1)
        got = lax.ppermute(sent, "xline", swap)
        return jnp.where(
            half == 0, jnp.concatenate([kept, got], axis=0), jnp.concatenate([got, kept], axis=0)
        )

    pieces = n_xline
    columns = lax.all_to_all(
        raw.reshape(n_i, n_x, pieces, depth // pieces).transpose(2, 0, 1, 3),
        "xline", split_axis=0, concat_axis=0, tiled=True,
    ).reshape(n_xline // 2, 2, n_i, n_x, depth // pieces)
    columns = jnp.where(core % 2 == 0, columns, columns[:, ::-1])
    positions = jnp.arange(full_x).astype(jnp.float32)
    weights = jnp.exp(-jnp.abs(positions[:, None] - positions[None, :]) / SMOOTH)
    weights = weights / jnp.sum(weights, axis=1, keepdims=True)
    gradient = jnp.einsum(
        "phixz,ypx->zhiy", columns, weights.reshape(full_x, n_xline // 2, n_x),
        precision=lax.Precision.HIGHEST,
    ).reshape(depth // pieces, tile_i, full_x)
    return gradient, split_pair(last), split_pair(previous)


def solution(mesh):
    return jax.shard_map(
        per_device,
        mesh=mesh,
        in_specs=(
            P(("shots", "inline"), "xline", None),
            P(("shots", "inline"), "xline", None),
            P(("shots", "inline"), "xline", None),
            P(("shots", "inline"), "xline", None),
            P("inline", "xline", None),
            P("inline", "xline", None),
            P("shots", ("xline", "inline")),
            P(("xline", "inline"), None),
            P(("xline", "inline"), None),
            P("shots"),
            P("shots", None),
        ),
        out_specs=(
            P(("shots", "xline"), "inline", None),
            P(("shots", "inline"), "xline", None),
            P(("shots", "inline"), "xline", None),
        ),
        check_vma=False,
    )
```

```python
import functools

import jax
import jax.numpy as jnp
from jax import lax
from jax.experimental import pallas as pl
from jax.experimental.pallas import tpu as pltpu
from jax.sharding import PartitionSpec as P

CAP = 8
SMOOTH = 16
MESH = pl.DeviceIdType.MESH

SECOND_COEFFS = (-205.0 / 72.0, 8.0 / 5.0, -1.0 / 5.0, 8.0 / 315.0, -1.0 / 560.0)
FIRST_COEFFS = (4.0 / 5.0, -1.0 / 5.0, 4.0 / 105.0, -1.0 / 280.0)
LEFT, RIGHT, UP, DOWN = 0, 1, 2, 3
DENSITY = 4


def split_bf16(value):
    high = value.astype(jnp.bfloat16)
    low = (value - high.astype(jnp.float32)).astype(jnp.bfloat16)
    return high, low


def dot(a, b):
    return jnp.dot(a, b, preferred_element_type=jnp.float32)


def wave_kernel(
    sizes,
    fwd_now, fwd_before, adj_now, adj_before, velocity, density,
    traces, rec_row, rec_row_t, rec_z, rec_live, src_row, src_z, wavelet,
    raw_out, last_out, previous_out,
    field, x_in, x_out, accel, base, image, slopes, speed_sq,
    row_map, row_map_t, z_map, z_high, z_low, residual_ref,
    landing, send_sem, recv_sem, swap_send, swap_recv,
):
    n_i, n_x, depth, steps, n_xline, n_inline = sizes
    rows = n_i * n_x
    xl = lax.axis_index("xline")
    core = lax.axis_index("inline")
    side = lax.rem(xl, 2)
    half = lax.rem(side + lax.rem(core, 2), 2)
    mate = xl + 1 - 2 * side
    has = (
        xl >= 2,
        xl < n_xline - 2,
        core * 2 + half > 0,
        core * 2 + half < 2 * n_inline - 1,
    )
    target = (
        {"xline": xl - 2},
        {"xline": xl + 2},
        {"xline": jnp.where(half == 1, mate, xl), "inline": jnp.where(half == 1, core, core - 1)},
        {"xline": jnp.where(half == 0, mate, xl), "inline": jnp.where(half == 0, core, core + 1)},
    )
    inner_x = pl.ds(8, n_x)

    middle = n_i // 2

    def copy_of(idx, way, part):
        part_rows = pl.ds(part * middle, middle)
        sem = way
        if way == LEFT:
            src, dst = x_out.at[idx, 0, part_rows], x_in.at[idx, 1, part_rows]
            sem = way + 4 * part
        elif way == RIGHT:
            src, dst = x_out.at[idx, 1, part_rows], x_in.at[idx, 0, part_rows]
            sem = way + 4 * part
        elif way == UP:
            src = field.at[idx, pl.ds(4, 4), inner_x, :]
            dst = field.at[idx, pl.ds(n_i + 4, 4), inner_x, :]
        else:
            src = field.at[idx, pl.ds(n_i, 4), inner_x, :]
            dst = field.at[idx, pl.ds(0, 4), inner_x, :]
        return pltpu.make_async_remote_copy(
            src_ref=src, dst_ref=dst,
            send_sem=send_sem.at[idx, sem], recv_sem=recv_sem.at[idx, sem],
            device_id=target[way], device_id_type=MESH,
        )

    def send(idx, part):
        part_rows = pl.ds(part * middle, middle)
        field_rows = pl.ds(4 + part * middle, middle)
        x_out[idx, 0, part_rows] = field[idx, field_rows, pl.ds(8, 4), :]
        x_out[idx, 1, part_rows] = field[idx, field_rows, pl.ds(4 + n_x, 4), :]
        for way in (LEFT, RIGHT, UP + part):
            @pl.when(has[way])
            def _():
                copy_of(idx, way, part).start()

    def finish(idx, part):
        for way in (LEFT, RIGHT, UP + part):
            @pl.when(has[way])
            def _():
                copy_of(idx, way, part).wait_send()
                copy_of(idx, way ^ 1, part).wait_recv()
        part_rows = pl.ds(part * middle, middle)
        field_rows = pl.ds(4 + part * middle, middle)
        field[idx, field_rows, pl.ds(4, 4), :] = x_in[idx, 0, part_rows]
        field[idx, field_rows, pl.ds(8 + n_x, 4), :] = x_in[idx, 1, part_rows]

    tile_x = n_x // 2
    own_x = pl.ds(pl.multiple_of(8 + tile_x * side, 8), tile_x)
    mate_x = pl.ds(pl.multiple_of(8 + tile_x * (1 - side), 8), tile_x)

    def swap_of(which, idx):
        return pltpu.make_async_remote_copy(
            src_ref=field.at[idx, pl.ds(4, n_i), mate_x, :], dst_ref=landing.at[which],
            send_sem=swap_send.at[which], recv_sem=swap_recv.at[which],
            device_id={"xline": mate}, device_id_type=MESH,
        )

    for idx in range(5):
        field[idx, pl.ds(0, 4)] = jnp.zeros((4,) + field.shape[2:], jnp.float32)
        field[idx, pl.ds(n_i + 4, 4)] = jnp.zeros((4,) + field.shape[2:], jnp.float32)
    x_in[...] = jnp.zeros(x_in.shape, jnp.float32)

    barrier = pltpu.get_barrier_semaphore()
    for way in range(4):
        @pl.when(has[way])
        def _():
            pl.semaphore_signal(barrier, inc=1, device_id=target[way], device_id_type=MESH)
    pl.semaphore_wait(barrier, sum(present.astype(jnp.int32) for present in has))

    inner_i = pl.ds(4, n_i)
    field[DENSITY, inner_i, inner_x, :] = density[...]
    field[0, inner_i, inner_x, :] = fwd_now[...]
    send(DENSITY, 0)
    send(DENSITY, 1)
    send(0, 0)
    send(0, 1)
    field[2, inner_i, inner_x, :] = adj_now[...]
    send(2, 0)
    send(2, 1)
    field[1, inner_i, inner_x, :] = fwd_before[...]
    field[3, inner_i, inner_x, :] = adj_before[...]

    speed_sq[...] = velocity[...] * velocity[...]
    image[...] = jnp.zeros(image.shape, jnp.float32)
    slots = rec_row.shape[0]
    row_map[...] = (lax.broadcasted_iota(jnp.int32, (rows, slots), 0) == rec_row_t[...]).astype(jnp.float32).astype(jnp.bfloat16)
    row_map_t[...] = (lax.broadcasted_iota(jnp.int32, (slots, rows), 1) == rec_row[...]).astype(jnp.float32).astype(jnp.bfloat16)
    z_map[...] = (lax.broadcasted_iota(jnp.int32, (slots, depth), 1) == rec_z[...]).astype(jnp.float32)
    src_rows = (lax.broadcasted_iota(jnp.int32, (rows, src_row.shape[1]), 0) == src_row[...]).astype(jnp.float32)
    src_cols = (lax.broadcasted_iota(jnp.int32, (src_z.shape[0], depth), 1) == src_z[...]).astype(jnp.float32).astype(jnp.bfloat16)
    offset = lax.broadcasted_iota(jnp.int32, (depth, depth), 0) - lax.broadcasted_iota(jnp.int32, (depth, depth), 1)
    second = jnp.where(offset == 0, 3.0 * SECOND_COEFFS[0], 0.0)
    first = jnp.zeros((depth, depth), jnp.float32)
    for k in range(1, 5):
        second = jnp.where((offset == k) | (offset == -k), SECOND_COEFFS[k], second)
        first = jnp.where(offset == k, FIRST_COEFFS[k - 1], first)
        first = jnp.where(offset == -k, -FIRST_COEFFS[k - 1], first)
    high, low = split_bf16(second)
    z_high[:, pl.ds(0, depth)] = high
    z_low[:, pl.ds(0, depth)] = low
    high, low = split_bf16(first)
    z_high[:, pl.ds(depth, depth)] = high
    z_low[:, pl.ds(depth, depth)] = low

    def flat(idx):
        return field[idx, inner_i, inner_x, :].reshape(rows, depth)

    def along_depth(idx):
        high, low = split_bf16(flat(idx))
        both = dot(high, z_high[...]) + (dot(low, z_high[...]) + dot(high, z_low[...]))
        return both[:, :depth], both[:, depth:]

    def across(idx, i):
        lap = slope_i = slope_x = None
        for k in range(1, 5):
            plus_i = field[idx, i + 4 + k, inner_x, :]
            minus_i = field[idx, i + 4 - k, inner_x, :]
            plus_x = field[idx, i + 4, pl.ds(8 + k, n_x), :]
            minus_x = field[idx, i + 4, pl.ds(8 - k, n_x), :]
            terms = (
                SECOND_COEFFS[k] * ((plus_i + minus_i) + (plus_x + minus_x)),
                FIRST_COEFFS[k - 1] * (plus_i - minus_i),
                FIRST_COEFFS[k - 1] * (plus_x - minus_x),
            )
            if lap is None:
                lap, slope_i, slope_x = terms
            else:
                lap, slope_i, slope_x = lap + terms[0], slope_i + terms[1], slope_x + terms[2]
        return lap, slope_i, slope_x

    def prepare(idx, term):
        lap, slope = along_depth(idx)
        partial = term + speed_sq[...].reshape(rows, depth) * (lap - slopes[2].reshape(rows, depth) * slope)
        base[...] = partial.reshape(n_i, n_x, depth)

    slopes[2] = along_depth(DENSITY)[1].reshape(n_i, n_x, depth)
    finish(DENSITY, 0)
    finish(DENSITY, 1)

    @pl.loop(0, n_i)
    def _(i):
        _, slope_i, slope_x = across(DENSITY, i)
        slopes[0, i] = slope_i
        slopes[1, i] = slope_x

    @pl.loop(0, steps)
    def _(t):
        now = lax.rem(t, 2)
        other = 1 - now
        high, low = split_bf16(src_rows * wavelet[pl.ds(t, 1), :])
        prepare(now, dot(high, src_cols) + dot(low, src_cols))

        for part in range(2):
            finish(now, part)

            @pl.loop(part * middle, (part + 1) * middle)
            def _(i):
                lap, slope_i, slope_x = across(now, i)
                change = base[i] + speed_sq[i] * (lap - slopes[0, i] * slope_i - slopes[1, i] * slope_x)
                accel[t, i] = change
                field[other, i + 4, inner_x, :] = (
                    2.0 * field[now, i + 4, inner_x, :] - field[other, i + 4, inner_x, :] + change
                )

            @pl.when(t < steps - 1)
            def _():
                send(other, part)

        high, low = split_bf16(flat(other))
        picked = dot(row_map_t[...], high) + dot(row_map_t[...], low)
        predicted = jnp.sum(picked * z_map[...], axis=1, keepdims=True)
        column = lax.broadcasted_iota(jnp.int32, traces.shape, 1) == t
        seen = jnp.sum(jnp.where(column, traces[...], 0.0), axis=1, keepdims=True)
        residual_ref[t] = rec_live[...] * (predicted - seen)

    @pl.loop(0, steps)
    def _(j):
        now = 2 + lax.rem(j, 2)
        other = 5 - now
        t = steps - 1 - j

        @pl.when(j == steps - 1)
        def _():
            swap_of(1, now).start()

        high, low = split_bf16(residual_ref[t] * z_map[...])
        prepare(now, dot(row_map[...], high) + dot(row_map[...], low))

        for part in range(2):
            finish(now, part)

            @pl.loop(part * middle, (part + 1) * middle)
            def _(i):
                lap, slope_i, slope_x = across(now, i)
                change = base[i] + speed_sq[i] * (lap - slopes[0, i] * slope_i - slopes[1, i] * slope_x)
                fresh = 2.0 * field[now, i + 4, inner_x, :] - field[other, i + 4, inner_x, :] + change
                field[other, i + 4, inner_x, :] = fresh
                image[i] += fresh * accel[t, i]

            @pl.when(j < steps - 1)
            def _():
                send(other, part)

    final = 2 + steps % 2
    swap_of(0, final).start()
    raw_out[...] = image[...] * (2.0 / steps) / velocity[...]
    own_rows, mate_rows = pl.ds(half * n_i, n_i), pl.ds((1 - half) * n_i, n_i)
    last_out[own_rows] = field[final, inner_i, own_x, :]
    previous_out[own_rows] = field[5 - final, inner_i, own_x, :]
    swap_of(1, 5 - final).wait()
    previous_out[mate_rows] = landing[1]
    swap_of(0, final).wait()
    last_out[mate_rows] = landing[0]


def per_device(
    fwd_now, fwd_before, adj_now, adj_before, velocity, log_density,
    observed, rec_cells, rec_counts, src_cell, wavelet,
):
    tile_i, tile_x, depth = fwd_now.shape
    steps = wavelet.shape[0]
    n_xline = lax.axis_size("xline")
    n_inline = lax.axis_size("inline")
    full_x = tile_x * n_xline
    n_i, n_x = tile_i // 2, tile_x * 2
    xl = lax.axis_index("xline")
    core = lax.axis_index("inline")
    side = xl % 2
    half = (side + core) % 2
    swap = [(k, k ^ 1) for k in range(n_xline)]

    def pair_up(mine, theirs, axis):
        return jnp.where(
            side == 0,
            jnp.concatenate([mine, theirs], axis=axis),
            jnp.concatenate([theirs, mine], axis=axis),
        )

    def gather_pair(value):
        kept = lax.dynamic_slice_in_dim(value, half * n_i, n_i, axis=0)
        sent = lax.dynamic_slice_in_dim(value, (1 - half) * n_i, n_i, axis=0)
        return pair_up(kept, lax.ppermute(sent, "xline", swap), 1)

    routed = lax.all_to_all(observed, ("xline", "inline"), split_axis=1, concat_axis=1, tiled=True)
    live = (jnp.arange(CAP)[None, :] < rec_counts[0][:, None]).astype(jnp.int32).reshape(1, -1)
    lists = jnp.concatenate([rec_cells, live], axis=0)
    lists = pair_up(lists, lax.ppermute(lists, "xline", swap), 1)
    traces = pair_up(routed, lax.ppermute(routed, "xline", swap), 1).T
    cells = lists[0]
    slots = cells.shape[0]
    cell_i = cells // (tile_x * depth) - half * n_i
    cell_x = cells // depth % tile_x + jnp.where(jnp.arange(slots) < slots // 2, 0, tile_x)
    rec_row = jnp.where((cell_i >= 0) & (cell_i < n_i), cell_i * n_x + cell_x, -1)
    rec_z = cells % depth
    src_i = src_cell // (full_x * depth) - (core * tile_i + half * n_i)
    src_x = src_cell // depth % full_x - (xl // 2) * n_x
    inside = (src_i >= 0) & (src_i < n_i) & (src_x >= 0) & (src_x < n_x)
    src_row = jnp.where(inside, src_i * n_x + src_x, -1)
    src_z = src_cell % depth

    block = (n_i, n_x, depth)
    rows = n_i * n_x
    vmem = pl.BlockSpec(memory_space=pltpu.VMEM)
    kernel = functools.partial(wave_kernel, (n_i, n_x, depth, steps, n_xline, n_inline))
    raw, last, previous = pl.pallas_call(
        kernel,
        out_shape=[jax.ShapeDtypeStruct(shape, jnp.float32) for shape in (block, fwd_now.shape, fwd_now.shape)],
        in_specs=[vmem] * 14,
        out_specs=[vmem] * 3,
        scratch_shapes=[
            pltpu.VMEM((5, n_i + 8, n_x + 16, depth), jnp.float32),
            pltpu.VMEM((5, 2, n_i, 4, depth), jnp.float32),
            pltpu.VMEM((5, 2, n_i, 4, depth), jnp.float32),
            pltpu.VMEM((steps,) + block, jnp.float32),
            pltpu.VMEM(block, jnp.float32),
            pltpu.VMEM(block, jnp.float32),
            pltpu.VMEM((3,) + block, jnp.float32),
            pltpu.VMEM(block, jnp.float32),
            pltpu.VMEM((rows, slots), jnp.bfloat16),
            pltpu.VMEM((slots, rows), jnp.bfloat16),
            pltpu.VMEM((slots, depth), jnp.float32),
            pltpu.VMEM((depth, 2 * depth), jnp.bfloat16),
            pltpu.VMEM((depth, 2 * depth), jnp.bfloat16),
            pltpu.VMEM((steps, slots, 1), jnp.float32),
            pltpu.VMEM((2, n_i, tile_x, depth), jnp.float32),
            pltpu.SemaphoreType.DMA((5, 6)),
            pltpu.SemaphoreType.DMA((5, 6)),
            pltpu.SemaphoreType.DMA((2,)),
            pltpu.SemaphoreType.DMA((2,)),
        ],
        compiler_params=pltpu.CompilerParams(
            collective_id=0, has_side_effects=True, vmem_limit_bytes=56 * 1024 * 1024
        ),
    )(
        gather_pair(fwd_now), gather_pair(fwd_before), gather_pair(adj_now), gather_pair(adj_before),
        gather_pair(velocity), gather_pair(log_density),
        traces, rec_row[:, None], rec_row[None, :], rec_z[:, None],
        lists[1].astype(jnp.float32)[:, None], src_row[None, :], src_z[:, None], wavelet,
    )

    pieces = n_xline
    columns = lax.all_to_all(
        raw.reshape(n_i, n_x, pieces, depth // pieces).transpose(2, 0, 1, 3),
        "xline", split_axis=0, concat_axis=0, tiled=True,
    ).reshape(n_xline // 2, 2, n_i, n_x, depth // pieces)
    columns = jnp.where(core % 2 == 0, columns, columns[:, ::-1])
    positions = jnp.arange(full_x).astype(jnp.float32)
    weights = jnp.exp(-jnp.abs(positions[:, None] - positions[None, :]) / SMOOTH)
    weights = weights / jnp.sum(weights, axis=1, keepdims=True)
    gradient = jnp.einsum(
        "phixz,ypx->zhiy", columns, weights.reshape(full_x, n_xline // 2, n_x),
        precision=lax.Precision.HIGHEST,
    ).reshape(depth // pieces, tile_i, full_x)
    return gradient, last, previous


def solution(mesh):
    return jax.shard_map(
        per_device,
        mesh=mesh,
        in_specs=(
            P(("shots", "inline"), "xline", None),
            P(("shots", "inline"), "xline", None),
            P(("shots", "inline"), "xline", None),
            P(("shots", "inline"), "xline", None),
            P("inline", "xline", None),
            P("inline", "xline", None),
            P("shots", ("xline", "inline")),
            P(("xline", "inline"), None),
            P(("xline", "inline"), None),
            P("shots"),
            P("shots", None),
        ),
        out_specs=(
            P(("shots", "xline"), "inline", None),
            P(("shots", "inline"), "xline", None),
            P(("shots", "inline"), "xline", None),
        ),
        check_vma=False,
    )
```

```python
import functools

import jax
import jax.numpy as jnp
from jax import lax
from jax.experimental import pallas as pl
from jax.experimental.pallas import tpu as pltpu
from jax.sharding import PartitionSpec as P

CAP = 8
SMOOTH = 16
MESH = pl.DeviceIdType.MESH

SECOND_COEFFS = (-205.0 / 72.0, 8.0 / 5.0, -1.0 / 5.0, 8.0 / 315.0, -1.0 / 560.0)
FIRST_COEFFS = (4.0 / 5.0, -1.0 / 5.0, 4.0 / 105.0, -1.0 / 280.0)
LEFT, RIGHT, UP, DOWN = 0, 1, 2, 3
DENSITY = 4


def split_bf16(value):
    high = value.astype(jnp.bfloat16)
    low = (value - high.astype(jnp.float32)).astype(jnp.bfloat16)
    return high, low


def dot(a, b):
    return jnp.dot(a, b, preferred_element_type=jnp.float32)


def wave_kernel(
    sizes,
    fwd_now, fwd_before, adj_now, adj_before, velocity, density,
    traces, rec_row, rec_row_t, rec_z, rec_live, src_row, src_z, wavelet,
    raw_out, last_out, previous_out,
    field, x_in, x_out, accel, base, image, slopes, speed_sq,
    row_map, row_map_t, z_map, z_high, z_low, residual_ref,
    speed, send_sem, recv_sem, swap_send, swap_recv,
):
    n_i, n_x, depth, steps, n_xline, n_inline = sizes
    rows = n_i * n_x
    xl = lax.axis_index("xline")
    core = lax.axis_index("inline")
    side = lax.rem(xl, 2)
    half = lax.rem(side + lax.rem(core, 2), 2)
    mate = xl + 1 - 2 * side
    has = (
        xl >= 2,
        xl < n_xline - 2,
        core * 2 + half > 0,
        core * 2 + half < 2 * n_inline - 1,
    )
    target = (
        {"xline": xl - 2},
        {"xline": xl + 2},
        {"xline": jnp.where(half == 1, mate, xl), "inline": jnp.where(half == 1, core, core - 1)},
        {"xline": jnp.where(half == 0, mate, xl), "inline": jnp.where(half == 0, core, core + 1)},
    )
    inner_x = pl.ds(8, n_x)

    middle = n_i // 2

    def copy_of(idx, way, part):
        part_rows = pl.ds(part * middle, middle)
        sem = way
        if way == LEFT:
            src, dst = x_out.at[idx, 0, part_rows], x_in.at[idx, 1, part_rows]
            sem = way + 4 * part
        elif way == RIGHT:
            src, dst = x_out.at[idx, 1, part_rows], x_in.at[idx, 0, part_rows]
            sem = way + 4 * part
        elif way == UP:
            src = field.at[idx, pl.ds(4, 4), inner_x, :]
            dst = field.at[idx, pl.ds(n_i + 4, 4), inner_x, :]
        else:
            src = field.at[idx, pl.ds(n_i, 4), inner_x, :]
            dst = field.at[idx, pl.ds(0, 4), inner_x, :]
        return pltpu.make_async_remote_copy(
            src_ref=src, dst_ref=dst,
            send_sem=send_sem.at[idx, sem], recv_sem=recv_sem.at[idx, sem],
            device_id=target[way], device_id_type=MESH,
        )

    def send(idx, part):
        part_rows = pl.ds(part * middle, middle)
        field_rows = pl.ds(4 + part * middle, middle)
        x_out[idx, 0, part_rows] = field[idx, field_rows, pl.ds(8, 4), :]
        x_out[idx, 1, part_rows] = field[idx, field_rows, pl.ds(4 + n_x, 4), :]
        for way in (LEFT, RIGHT, UP + part):
            @pl.when(has[way])
            def _():
                copy_of(idx, way, part).start()

    def finish(idx, part):
        for way in (LEFT, RIGHT, UP + part):
            @pl.when(has[way])
            def _():
                copy_of(idx, way, part).wait_send()
                copy_of(idx, way ^ 1, part).wait_recv()
        part_rows = pl.ds(part * middle, middle)
        field_rows = pl.ds(4 + part * middle, middle)
        field[idx, field_rows, pl.ds(4, 4), :] = x_in[idx, 0, part_rows]
        field[idx, field_rows, pl.ds(8 + n_x, 4), :] = x_in[idx, 1, part_rows]

    for idx in range(5):
        field[idx, pl.ds(0, 4)] = jnp.zeros((4,) + field.shape[2:], jnp.float32)
        field[idx, pl.ds(n_i + 4, 4)] = jnp.zeros((4,) + field.shape[2:], jnp.float32)
    x_in[...] = jnp.zeros(x_in.shape, jnp.float32)

    barrier = pltpu.get_barrier_semaphore()
    for way in range(4):
        @pl.when(has[way])
        def _():
            pl.semaphore_signal(barrier, inc=1, device_id=target[way], device_id_type=MESH)
    pl.semaphore_wait(barrier, sum(present.astype(jnp.int32) for present in has))

    inner_i = pl.ds(4, n_i)
    tile_x = n_x // 2
    kept, sent = pl.ds(half * n_i, n_i), pl.ds((1 - half) * n_i, n_i)
    own_x = pl.ds(pl.multiple_of(8 + tile_x * side, 8), tile_x)
    inputs = (fwd_now, fwd_before, adj_now, adj_before, density)

    def swap_of(which):
        if which < 5:
            src, dst = inputs[which].at[sent], field.at[which, inner_i, own_x, :]
        else:
            src = velocity.at[sent]
            dst = speed.at[:, pl.ds(pl.multiple_of(tile_x * side, 8), tile_x), :]
        return pltpu.make_async_remote_copy(
            src_ref=src, dst_ref=dst,
            send_sem=swap_send.at[which], recv_sem=swap_recv.at[which],
            device_id={"xline": mate}, device_id_type=MESH,
        )

    for which in (DENSITY, 0, 5, 1, 2, 3):
        swap_of(which).start()
    for which in (DENSITY, 0, 1, 2, 3):
        field[which, inner_i, own_x, :] = inputs[which][kept]
    speed[:, pl.ds(pl.multiple_of(tile_x * side, 8), tile_x), :] = velocity[kept]
    for which in (DENSITY, 0):
        swap_of(which).wait()
        send(which, 0)
        send(which, 1)

    image[...] = jnp.zeros(image.shape, jnp.float32)
    slots = rec_row.shape[0]
    row_map[...] = (lax.broadcasted_iota(jnp.int32, (rows, slots), 0) == rec_row_t[...]).astype(jnp.float32).astype(jnp.bfloat16)
    row_map_t[...] = (lax.broadcasted_iota(jnp.int32, (slots, rows), 1) == rec_row[...]).astype(jnp.float32).astype(jnp.bfloat16)
    z_map[...] = (lax.broadcasted_iota(jnp.int32, (slots, depth), 1) == rec_z[...]).astype(jnp.float32)
    src_rows = (lax.broadcasted_iota(jnp.int32, (rows, src_row.shape[1]), 0) == src_row[...]).astype(jnp.float32)
    src_cols = (lax.broadcasted_iota(jnp.int32, (src_z.shape[0], depth), 1) == src_z[...]).astype(jnp.float32).astype(jnp.bfloat16)
    offset = lax.broadcasted_iota(jnp.int32, (depth, depth), 0) - lax.broadcasted_iota(jnp.int32, (depth, depth), 1)
    second = jnp.where(offset == 0, 3.0 * SECOND_COEFFS[0], 0.0)
    first = jnp.zeros((depth, depth), jnp.float32)
    for k in range(1, 5):
        second = jnp.where((offset == k) | (offset == -k), SECOND_COEFFS[k], second)
        first = jnp.where(offset == k, FIRST_COEFFS[k - 1], first)
        first = jnp.where(offset == -k, -FIRST_COEFFS[k - 1], first)
    high, low = split_bf16(second)
    z_high[:, pl.ds(0, depth)] = high
    z_low[:, pl.ds(0, depth)] = low
    high, low = split_bf16(first)
    z_high[:, pl.ds(depth, depth)] = high
    z_low[:, pl.ds(depth, depth)] = low

    def flat(idx):
        return field[idx, inner_i, inner_x, :].reshape(rows, depth)

    def along_depth(idx):
        high, low = split_bf16(flat(idx))
        both = dot(high, z_high[...]) + (dot(low, z_high[...]) + dot(high, z_low[...]))
        return both[:, :depth], both[:, depth:]

    def across(idx, i):
        lap = slope_i = slope_x = None
        for k in range(1, 5):
            plus_i = field[idx, i + 4 + k, inner_x, :]
            minus_i = field[idx, i + 4 - k, inner_x, :]
            plus_x = field[idx, i + 4, pl.ds(8 + k, n_x), :]
            minus_x = field[idx, i + 4, pl.ds(8 - k, n_x), :]
            terms = (
                SECOND_COEFFS[k] * ((plus_i + minus_i) + (plus_x + minus_x)),
                FIRST_COEFFS[k - 1] * (plus_i - minus_i),
                FIRST_COEFFS[k - 1] * (plus_x - minus_x),
            )
            if lap is None:
                lap, slope_i, slope_x = terms
            else:
                lap, slope_i, slope_x = lap + terms[0], slope_i + terms[1], slope_x + terms[2]
        return lap, slope_i, slope_x

    def prepare(idx, term):
        lap, slope = along_depth(idx)
        partial = term + speed_sq[...].reshape(rows, depth) * (lap - slopes[2].reshape(rows, depth) * slope)
        base[...] = partial.reshape(n_i, n_x, depth)

    swap_of(5).wait()
    speed_sq[...] = speed[...] * speed[...]
    for which in (1, 2, 3):
        swap_of(which).wait()
    slopes[2] = along_depth(DENSITY)[1].reshape(n_i, n_x, depth)
    finish(DENSITY, 0)
    finish(DENSITY, 1)

    @pl.loop(0, n_i)
    def _(i):
        _, slope_i, slope_x = across(DENSITY, i)
        slopes[0, i] = slope_i
        slopes[1, i] = slope_x

    send(2, 0)
    send(2, 1)

    @pl.loop(0, steps)
    def _(t):
        now = lax.rem(t, 2)
        other = 1 - now
        high, low = split_bf16(src_rows * wavelet[pl.ds(t, 1), :])
        prepare(now, dot(high, src_cols) + dot(low, src_cols))

        for part in range(2):
            finish(now, part)

            @pl.loop(part * middle, (part + 1) * middle)
            def _(i):
                lap, slope_i, slope_x = across(now, i)
                change = base[i] + speed_sq[i] * (lap - slopes[0, i] * slope_i - slopes[1, i] * slope_x)
                accel[t, i] = change
                field[other, i + 4, inner_x, :] = (
                    2.0 * field[now, i + 4, inner_x, :] - field[other, i + 4, inner_x, :] + change
                )

            @pl.when(t < steps - 1)
            def _():
                send(other, part)

        high, low = split_bf16(flat(other))
        picked = dot(row_map_t[...], high) + dot(row_map_t[...], low)
        predicted = jnp.sum(picked * z_map[...], axis=1, keepdims=True)
        column = lax.broadcasted_iota(jnp.int32, traces.shape, 1) == t
        seen = jnp.sum(jnp.where(column, traces[...], 0.0), axis=1, keepdims=True)
        residual_ref[t] = rec_live[...] * (predicted - seen)

    @pl.loop(0, steps)
    def _(j):
        now = 2 + lax.rem(j, 2)
        other = 5 - now
        t = steps - 1 - j
        high, low = split_bf16(residual_ref[t] * z_map[...])
        prepare(now, dot(row_map[...], high) + dot(row_map[...], low))

        for part in range(2):
            finish(now, part)

            @pl.loop(part * middle, (part + 1) * middle)
            def _(i):
                lap, slope_i, slope_x = across(now, i)
                change = base[i] + speed_sq[i] * (lap - slopes[0, i] * slope_i - slopes[1, i] * slope_x)
                fresh = 2.0 * field[now, i + 4, inner_x, :] - field[other, i + 4, inner_x, :] + change
                field[other, i + 4, inner_x, :] = fresh
                image[i] += fresh * accel[t, i]

            @pl.when(j < steps - 1)
            def _():
                send(other, part)

    raw_out[...] = image[...] * (2.0 / steps) / speed[...]
    last_out[...] = field[2 + steps % 2, inner_i, inner_x, :]
    previous_out[...] = field[2 + (steps - 1) % 2, inner_i, inner_x, :]


def per_device(
    fwd_now, fwd_before, adj_now, adj_before, velocity, log_density,
    observed, rec_cells, rec_counts, src_cell, wavelet,
):
    tile_i, tile_x, depth = fwd_now.shape
    steps = wavelet.shape[0]
    n_xline = lax.axis_size("xline")
    n_inline = lax.axis_size("inline")
    full_x = tile_x * n_xline
    n_i, n_x = tile_i // 2, tile_x * 2
    xl = lax.axis_index("xline")
    core = lax.axis_index("inline")
    side = xl % 2
    half = (side + core) % 2
    swap = [(k, k ^ 1) for k in range(n_xline)]

    def pair_up(mine, theirs, axis):
        return jnp.where(
            side == 0,
            jnp.concatenate([mine, theirs], axis=axis),
            jnp.concatenate([theirs, mine], axis=axis),
        )

    routed = lax.all_to_all(observed, ("xline", "inline"), split_axis=1, concat_axis=1, tiled=True)
    live = (jnp.arange(CAP)[None, :] < rec_counts[0][:, None]).astype(jnp.int32).reshape(1, -1)
    lists = jnp.concatenate([rec_cells, live], axis=0)
    lists = pair_up(lists, lax.ppermute(lists, "xline", swap), 1)
    traces = pair_up(routed, lax.ppermute(routed, "xline", swap), 1).T
    cells = lists[0]
    slots = cells.shape[0]
    cell_i = cells // (tile_x * depth) - half * n_i
    cell_x = cells // depth % tile_x + jnp.where(jnp.arange(slots) < slots // 2, 0, tile_x)
    rec_row = jnp.where((cell_i >= 0) & (cell_i < n_i), cell_i * n_x + cell_x, -1)
    rec_z = cells % depth
    src_i = src_cell // (full_x * depth) - (core * tile_i + half * n_i)
    src_x = src_cell // depth % full_x - (xl // 2) * n_x
    inside = (src_i >= 0) & (src_i < n_i) & (src_x >= 0) & (src_x < n_x)
    src_row = jnp.where(inside, src_i * n_x + src_x, -1)
    src_z = src_cell % depth

    block = (n_i, n_x, depth)
    rows = n_i * n_x
    vmem = pl.BlockSpec(memory_space=pltpu.VMEM)
    kernel = functools.partial(wave_kernel, (n_i, n_x, depth, steps, n_xline, n_inline))
    raw, last, previous = pl.pallas_call(
        kernel,
        out_shape=[jax.ShapeDtypeStruct(block, jnp.float32)] * 3,
        in_specs=[vmem] * 14,
        out_specs=[vmem] * 3,
        scratch_shapes=[
            pltpu.VMEM((5, n_i + 8, n_x + 16, depth), jnp.float32),
            pltpu.VMEM((5, 2, n_i, 4, depth), jnp.float32),
            pltpu.VMEM((5, 2, n_i, 4, depth), jnp.float32),
            pltpu.VMEM((steps,) + block, jnp.float32),
            pltpu.VMEM(block, jnp.float32),
            pltpu.VMEM(block, jnp.float32),
            pltpu.VMEM((3,) + block, jnp.float32),
            pltpu.VMEM(block, jnp.float32),
            pltpu.VMEM((rows, slots), jnp.bfloat16),
            pltpu.VMEM((slots, rows), jnp.bfloat16),
            pltpu.VMEM((slots, depth), jnp.float32),
            pltpu.VMEM((depth, 2 * depth), jnp.bfloat16),
            pltpu.VMEM((depth, 2 * depth), jnp.bfloat16),
            pltpu.VMEM((steps, slots, 1), jnp.float32),
            pltpu.VMEM((n_i, n_x, depth), jnp.float32),
            pltpu.SemaphoreType.DMA((5, 6)),
            pltpu.SemaphoreType.DMA((5, 6)),
            pltpu.SemaphoreType.DMA((6,)),
            pltpu.SemaphoreType.DMA((6,)),
        ],
        compiler_params=pltpu.CompilerParams(
            collective_id=0, has_side_effects=True, vmem_limit_bytes=56 * 1024 * 1024
        ),
    )(
        fwd_now, fwd_before, adj_now, adj_before, velocity, log_density,
        traces, rec_row[:, None], rec_row[None, :], rec_z[:, None],
        lists[1].astype(jnp.float32)[:, None], src_row[None, :], src_z[:, None], wavelet,
    )

    def split_pair(value):
        kept = lax.dynamic_slice_in_dim(value, side * tile_x, tile_x, axis=1)
        sent = lax.dynamic_slice_in_dim(value, (1 - side) * tile_x, tile_x, axis=1)
        got = lax.ppermute(sent, "xline", swap)
        return jnp.where(
            half == 0, jnp.concatenate([kept, got], axis=0), jnp.concatenate([got, kept], axis=0)
        )

    pieces = n_xline
    columns = lax.all_to_all(
        raw.reshape(n_i, n_x, pieces, depth // pieces).transpose(2, 0, 1, 3),
        "xline", split_axis=0, concat_axis=0, tiled=True,
    ).reshape(n_xline // 2, 2, n_i, n_x, depth // pieces)
    columns = jnp.where(core % 2 == 0, columns, columns[:, ::-1])
    positions = jnp.arange(full_x).astype(jnp.float32)
    weights = jnp.exp(-jnp.abs(positions[:, None] - positions[None, :]) / SMOOTH)
    weights = weights / jnp.sum(weights, axis=1, keepdims=True)
    gradient = jnp.einsum(
        "phixz,ypx->zhiy", columns, weights.reshape(full_x, n_xline // 2, n_x),
        precision=lax.Precision.HIGHEST,
    ).reshape(depth // pieces, tile_i, full_x)
    return gradient, split_pair(last), split_pair(previous)


def solution(mesh):
    return jax.shard_map(
        per_device,
        mesh=mesh,
        in_specs=(
            P(("shots", "inline"), "xline", None),
            P(("shots", "inline"), "xline", None),
            P(("shots", "inline"), "xline", None),
            P(("shots", "inline"), "xline", None),
            P("inline", "xline", None),
            P("inline", "xline", None),
            P("shots", ("xline", "inline")),
            P(("xline", "inline"), None),
            P(("xline", "inline"), None),
            P("shots"),
            P("shots", None),
        ),
        out_specs=(
            P(("shots", "xline"), "inline", None),
            P(("shots", "inline"), "xline", None),
            P(("shots", "inline"), "xline", None),
        ),
        check_vma=False,
    )
```

```python
import functools

import jax
import jax.numpy as jnp
from jax import lax
from jax.experimental import pallas as pl
from jax.experimental.pallas import tpu as pltpu
from jax.sharding import PartitionSpec as P

CAP = 8
SMOOTH = 16
MESH = pl.DeviceIdType.MESH

SECOND_COEFFS = (-205.0 / 72.0, 8.0 / 5.0, -1.0 / 5.0, 8.0 / 315.0, -1.0 / 560.0)
FIRST_COEFFS = (4.0 / 5.0, -1.0 / 5.0, 4.0 / 105.0, -1.0 / 280.0)
LEFT, RIGHT, UP, DOWN = 0, 1, 2, 3
DENSITY = 4


def split_bf16(value):
    high = value.astype(jnp.bfloat16)
    low = (value - high.astype(jnp.float32)).astype(jnp.bfloat16)
    return high, low


def dot(a, b):
    return jnp.dot(a, b, preferred_element_type=jnp.float32)


def wave_kernel(
    sizes,
    fwd_now, fwd_before, adj_now, adj_before, velocity, density,
    traces, rec_row, rec_row_t, rec_z, rec_live, src_row, src_z, wavelet,
    raw_out, last_out, previous_out,
    field, x_in, x_out, accel, base, image, slopes, speed_sq,
    row_map, row_map_t, z_map, z_high, z_low, residual_ref,
    speed, send_sem, recv_sem, swap_send, swap_recv,
):
    n_i, n_x, depth, steps, n_xline, n_inline = sizes
    rows = n_i * n_x
    xl = lax.axis_index("xline")
    core = lax.axis_index("inline")
    side = lax.rem(xl, 2)
    half = lax.rem(side + lax.rem(core, 2), 2)
    mate = xl + 1 - 2 * side
    has = (
        xl >= 2,
        xl < n_xline - 2,
        core * 2 + half > 0,
        core * 2 + half < 2 * n_inline - 1,
    )
    target = (
        {"xline": xl - 2},
        {"xline": xl + 2},
        {"xline": jnp.where(half == 1, mate, xl), "inline": jnp.where(half == 1, core, core - 1)},
        {"xline": jnp.where(half == 0, mate, xl), "inline": jnp.where(half == 0, core, core + 1)},
    )
    inner_x = pl.ds(8, n_x)

    middle = n_i // 2

    def copy_of(idx, way, part):
        part_rows = pl.ds(part * middle, middle)
        sem = way
        if way == LEFT:
            src, dst = x_out.at[idx, 0, part_rows], x_in.at[idx, 1, part_rows]
            sem = way + 4 * part
        elif way == RIGHT:
            src, dst = x_out.at[idx, 1, part_rows], x_in.at[idx, 0, part_rows]
            sem = way + 4 * part
        elif way == UP:
            src = field.at[idx, pl.ds(4, 4), inner_x, :]
            dst = field.at[idx, pl.ds(n_i + 4, 4), inner_x, :]
        else:
            src = field.at[idx, pl.ds(n_i, 4), inner_x, :]
            dst = field.at[idx, pl.ds(0, 4), inner_x, :]
        return pltpu.make_async_remote_copy(
            src_ref=src, dst_ref=dst,
            send_sem=send_sem.at[idx, sem], recv_sem=recv_sem.at[idx, sem],
            device_id=target[way], device_id_type=MESH,
        )

    def send(idx, part):
        part_rows = pl.ds(part * middle, middle)
        field_rows = pl.ds(4 + part * middle, middle)
        x_out[idx, 0, part_rows] = field[idx, field_rows, pl.ds(8, 4), :]
        x_out[idx, 1, part_rows] = field[idx, field_rows, pl.ds(4 + n_x, 4), :]
        for way in (LEFT, RIGHT, UP + part):
            @pl.when(has[way])
            def _():
                copy_of(idx, way, part).start()

    def finish(idx, part):
        for way in (LEFT, RIGHT, UP + part):
            @pl.when(has[way])
            def _():
                copy_of(idx, way, part).wait_send()
                copy_of(idx, way ^ 1, part).wait_recv()
        part_rows = pl.ds(part * middle, middle)
        field_rows = pl.ds(4 + part * middle, middle)
        field[idx, field_rows, pl.ds(4, 4), :] = x_in[idx, 0, part_rows]
        field[idx, field_rows, pl.ds(8 + n_x, 4), :] = x_in[idx, 1, part_rows]

    for idx in range(5):
        field[idx, pl.ds(0, 4)] = jnp.zeros((4,) + field.shape[2:], jnp.float32)
        field[idx, pl.ds(n_i + 4, 4)] = jnp.zeros((4,) + field.shape[2:], jnp.float32)
    x_in[...] = jnp.zeros(x_in.shape, jnp.float32)

    barrier = pltpu.get_barrier_semaphore()
    for way in range(4):
        @pl.when(has[way])
        def _():
            pl.semaphore_signal(barrier, inc=1, device_id=target[way], device_id_type=MESH)
    pl.semaphore_wait(barrier, sum(present.astype(jnp.int32) for present in has))

    inner_i = pl.ds(4, n_i)
    tile_x = n_x // 2
    kept, sent = pl.ds(half * n_i, n_i), pl.ds((1 - half) * n_i, n_i)
    own_x = pl.ds(pl.multiple_of(8 + tile_x * side, 8), tile_x)
    inputs = (fwd_now, fwd_before, adj_now, adj_before, density)

    def swap_of(which):
        if which < 5:
            src, dst = inputs[which].at[sent], field.at[which, inner_i, own_x, :]
        else:
            src = velocity.at[sent]
            dst = speed.at[:, pl.ds(pl.multiple_of(tile_x * side, 8), tile_x), :]
        return pltpu.make_async_remote_copy(
            src_ref=src, dst_ref=dst,
            send_sem=swap_send.at[which], recv_sem=swap_recv.at[which],
            device_id={"xline": mate}, device_id_type=MESH,
        )

    for which in (DENSITY, 0):
        swap_of(which).start()
    for which in (DENSITY, 0, 1, 2, 3):
        field[which, inner_i, own_x, :] = inputs[which][kept]
    speed[:, pl.ds(pl.multiple_of(tile_x * side, 8), tile_x), :] = velocity[kept]
    for which in (DENSITY, 0):
        swap_of(which).wait()
        send(which, 0)
        send(which, 1)
    for which in (5, 1):
        swap_of(which).start()

    image[...] = jnp.zeros(image.shape, jnp.float32)
    slots = rec_row.shape[0]
    row_map[...] = (lax.broadcasted_iota(jnp.int32, (rows, slots), 0) == rec_row_t[...]).astype(jnp.float32).astype(jnp.bfloat16)
    row_map_t[...] = (lax.broadcasted_iota(jnp.int32, (slots, rows), 1) == rec_row[...]).astype(jnp.float32).astype(jnp.bfloat16)
    z_map[...] = (lax.broadcasted_iota(jnp.int32, (slots, depth), 1) == rec_z[...]).astype(jnp.float32)
    src_rows = (lax.broadcasted_iota(jnp.int32, (rows, src_row.shape[1]), 0) == src_row[...]).astype(jnp.float32)
    src_cols = (lax.broadcasted_iota(jnp.int32, (src_z.shape[0], depth), 1) == src_z[...]).astype(jnp.float32).astype(jnp.bfloat16)
    offset = lax.broadcasted_iota(jnp.int32, (depth, depth), 0) - lax.broadcasted_iota(jnp.int32, (depth, depth), 1)
    second = jnp.where(offset == 0, 3.0 * SECOND_COEFFS[0], 0.0)
    first = jnp.zeros((depth, depth), jnp.float32)
    for k in range(1, 5):
        second = jnp.where((offset == k) | (offset == -k), SECOND_COEFFS[k], second)
        first = jnp.where(offset == k, FIRST_COEFFS[k - 1], first)
        first = jnp.where(offset == -k, -FIRST_COEFFS[k - 1], first)
    high, low = split_bf16(second)
    z_high[:, pl.ds(0, depth)] = high
    z_low[:, pl.ds(0, depth)] = low
    high, low = split_bf16(first)
    z_high[:, pl.ds(depth, depth)] = high
    z_low[:, pl.ds(depth, depth)] = low

    def flat(idx):
        return field[idx, inner_i, inner_x, :].reshape(rows, depth)

    def along_depth(idx):
        high, low = split_bf16(flat(idx))
        both = dot(high, z_high[...]) + (dot(low, z_high[...]) + dot(high, z_low[...]))
        return both[:, :depth], both[:, depth:]

    def across(idx, i):
        lap = slope_i = slope_x = None
        for k in range(1, 5):
            plus_i = field[idx, i + 4 + k, inner_x, :]
            minus_i = field[idx, i + 4 - k, inner_x, :]
            plus_x = field[idx, i + 4, pl.ds(8 + k, n_x), :]
            minus_x = field[idx, i + 4, pl.ds(8 - k, n_x), :]
            terms = (
                SECOND_COEFFS[k] * ((plus_i + minus_i) + (plus_x + minus_x)),
                FIRST_COEFFS[k - 1] * (plus_i - minus_i),
                FIRST_COEFFS[k - 1] * (plus_x - minus_x),
            )
            if lap is None:
                lap, slope_i, slope_x = terms
            else:
                lap, slope_i, slope_x = lap + terms[0], slope_i + terms[1], slope_x + terms[2]
        return lap, slope_i, slope_x

    def prepare(idx, term):
        lap, slope = along_depth(idx)
        partial = term + speed_sq[...].reshape(rows, depth) * (lap - slopes[2].reshape(rows, depth) * slope)
        base[...] = partial.reshape(n_i, n_x, depth)

    swap_of(5).wait()
    speed_sq[...] = speed[...] * speed[...]
    slopes[2] = along_depth(DENSITY)[1].reshape(n_i, n_x, depth)
    finish(DENSITY, 0)
    finish(DENSITY, 1)

    @pl.loop(0, n_i)
    def _(i):
        _, slope_i, slope_x = across(DENSITY, i)
        slopes[0, i] = slope_i
        slopes[1, i] = slope_x

    swap_of(1).wait()

    @pl.loop(0, steps)
    def _(t):
        now = lax.rem(t, 2)
        other = 1 - now
        for which in (2, 3):
            @pl.when(t == jnp.int32((which - 2) * steps // 4))
            def _():
                swap_of(which).start()

        high, low = split_bf16(src_rows * wavelet[pl.ds(t, 1), :])
        prepare(now, dot(high, src_cols) + dot(low, src_cols))

        for part in range(2):
            finish(now, part)

            @pl.loop(part * middle, (part + 1) * middle)
            def _(i):
                lap, slope_i, slope_x = across(now, i)
                change = base[i] + speed_sq[i] * (lap - slopes[0, i] * slope_i - slopes[1, i] * slope_x)
                accel[t, i] = change
                field[other, i + 4, inner_x, :] = (
                    2.0 * field[now, i + 4, inner_x, :] - field[other, i + 4, inner_x, :] + change
                )

            @pl.when(t < steps - 1)
            def _():
                send(other, part)

        @pl.when(t == steps - 1)
        def _():
            swap_of(2).wait()
            send(2, 0)
            send(2, 1)
            swap_of(3).wait()

        high, low = split_bf16(flat(other))
        picked = dot(row_map_t[...], high) + dot(row_map_t[...], low)
        predicted = jnp.sum(picked * z_map[...], axis=1, keepdims=True)
        column = lax.broadcasted_iota(jnp.int32, traces.shape, 1) == t
        seen = jnp.sum(jnp.where(column, traces[...], 0.0), axis=1, keepdims=True)
        residual_ref[t] = rec_live[...] * (predicted - seen)

    @pl.loop(0, steps)
    def _(j):
        now = 2 + lax.rem(j, 2)
        other = 5 - now
        t = steps - 1 - j
        high, low = split_bf16(residual_ref[t] * z_map[...])
        prepare(now, dot(row_map[...], high) + dot(row_map[...], low))

        for part in range(2):
            finish(now, part)

            @pl.loop(part * middle, (part + 1) * middle)
            def _(i):
                lap, slope_i, slope_x = across(now, i)
                change = base[i] + speed_sq[i] * (lap - slopes[0, i] * slope_i - slopes[1, i] * slope_x)
                fresh = 2.0 * field[now, i + 4, inner_x, :] - field[other, i + 4, inner_x, :] + change
                field[other, i + 4, inner_x, :] = fresh
                image[i] += fresh * accel[t, i]

            @pl.when(j < steps - 1)
            def _():
                send(other, part)

    raw_out[...] = image[...] * (2.0 / steps) / speed[...]
    last_out[...] = field[2 + steps % 2, inner_i, inner_x, :]
    previous_out[...] = field[2 + (steps - 1) % 2, inner_i, inner_x, :]


def per_device(
    fwd_now, fwd_before, adj_now, adj_before, velocity, log_density,
    observed, rec_cells, rec_counts, src_cell, wavelet,
):
    tile_i, tile_x, depth = fwd_now.shape
    steps = wavelet.shape[0]
    n_xline = lax.axis_size("xline")
    n_inline = lax.axis_size("inline")
    full_x = tile_x * n_xline
    n_i, n_x = tile_i // 2, tile_x * 2
    xl = lax.axis_index("xline")
    core = lax.axis_index("inline")
    side = xl % 2
    half = (side + core) % 2
    swap = [(k, k ^ 1) for k in range(n_xline)]

    def pair_up(mine, theirs, axis):
        return jnp.where(
            side == 0,
            jnp.concatenate([mine, theirs], axis=axis),
            jnp.concatenate([theirs, mine], axis=axis),
        )

    columns = observed.reshape(steps, n_xline // 2, 1, 2, n_inline, CAP).swapaxes(3, 4)
    columns = jnp.broadcast_to(columns, (steps, n_xline // 2, 2, n_inline, 2, CAP))
    routed = lax.all_to_all(
        columns.reshape(steps, -1), ("xline", "inline"), split_axis=1, concat_axis=1, tiled=True
    )
    live = (jnp.arange(CAP)[None, :] < rec_counts[0][:, None]).astype(jnp.int32).reshape(1, -1)
    lists = jnp.concatenate([rec_cells, live], axis=0)
    lists = pair_up(lists, lax.ppermute(lists, "xline", swap), 1)
    traces = routed.reshape(steps, -1, 2, CAP).transpose(2, 1, 3, 0).reshape(-1, steps)
    cells = lists[0]
    slots = cells.shape[0]
    cell_i = cells // (tile_x * depth) - half * n_i
    cell_x = cells // depth % tile_x + jnp.where(jnp.arange(slots) < slots // 2, 0, tile_x)
    rec_row = jnp.where((cell_i >= 0) & (cell_i < n_i), cell_i * n_x + cell_x, -1)
    rec_z = cells % depth
    src_i = src_cell // (full_x * depth) - (core * tile_i + half * n_i)
    src_x = src_cell // depth % full_x - (xl // 2) * n_x
    inside = (src_i >= 0) & (src_i < n_i) & (src_x >= 0) & (src_x < n_x)
    src_row = jnp.where(inside, src_i * n_x + src_x, -1)
    src_z = src_cell % depth

    block = (n_i, n_x, depth)
    rows = n_i * n_x
    vmem = pl.BlockSpec(memory_space=pltpu.VMEM)
    kernel = functools.partial(wave_kernel, (n_i, n_x, depth, steps, n_xline, n_inline))
    raw, last, previous = pl.pallas_call(
        kernel,
        out_shape=[jax.ShapeDtypeStruct(block, jnp.float32)] * 3,
        in_specs=[vmem] * 14,
        out_specs=[vmem] * 3,
        scratch_shapes=[
            pltpu.VMEM((5, n_i + 8, n_x + 16, depth), jnp.float32),
            pltpu.VMEM((5, 2, n_i, 4, depth), jnp.float32),
            pltpu.VMEM((5, 2, n_i, 4, depth), jnp.float32),
            pltpu.VMEM((steps,) + block, jnp.float32),
            pltpu.VMEM(block, jnp.float32),
            pltpu.VMEM(block, jnp.float32),
            pltpu.VMEM((3,) + block, jnp.float32),
            pltpu.VMEM(block, jnp.float32),
            pltpu.VMEM((rows, slots), jnp.bfloat16),
            pltpu.VMEM((slots, rows), jnp.bfloat16),
            pltpu.VMEM((slots, depth), jnp.float32),
            pltpu.VMEM((depth, 2 * depth), jnp.bfloat16),
            pltpu.VMEM((depth, 2 * depth), jnp.bfloat16),
            pltpu.VMEM((steps, slots, 1), jnp.float32),
            pltpu.VMEM((n_i, n_x, depth), jnp.float32),
            pltpu.SemaphoreType.DMA((5, 6)),
            pltpu.SemaphoreType.DMA((5, 6)),
            pltpu.SemaphoreType.DMA((6,)),
            pltpu.SemaphoreType.DMA((6,)),
        ],
        compiler_params=pltpu.CompilerParams(
            collective_id=0, has_side_effects=True, vmem_limit_bytes=56 * 1024 * 1024
        ),
    )(
        fwd_now, fwd_before, adj_now, adj_before, velocity, log_density,
        traces, rec_row[:, None], rec_row[None, :], rec_z[:, None],
        lists[1].astype(jnp.float32)[:, None], src_row[None, :], src_z[:, None], wavelet,
    )

    def split_pair(value):
        kept = lax.dynamic_slice_in_dim(value, side * tile_x, tile_x, axis=1)
        sent = lax.dynamic_slice_in_dim(value, (1 - side) * tile_x, tile_x, axis=1)
        got = lax.ppermute(sent, "xline", swap)
        return jnp.where(
            half == 0, jnp.concatenate([kept, got], axis=0), jnp.concatenate([got, kept], axis=0)
        )

    pieces = n_xline
    columns = lax.all_to_all(
        raw.reshape(n_i, n_x, pieces, depth // pieces).transpose(2, 0, 1, 3),
        "xline", split_axis=0, concat_axis=0, tiled=True,
    ).reshape(n_xline // 2, 2, n_i, n_x, depth // pieces)
    columns = jnp.where(core % 2 == 0, columns, columns[:, ::-1])
    positions = jnp.arange(full_x).astype(jnp.float32)
    weights = jnp.exp(-jnp.abs(positions[:, None] - positions[None, :]) / SMOOTH)
    weights = weights / jnp.sum(weights, axis=1, keepdims=True)
    gradient = jnp.einsum(
        "phixz,ypx->zhiy", columns, weights.reshape(full_x, n_xline // 2, n_x),
        precision=lax.Precision.HIGHEST,
    ).reshape(depth // pieces, tile_i, full_x)
    return gradient, split_pair(last), split_pair(previous)


def solution(mesh):
    return jax.shard_map(
        per_device,
        mesh=mesh,
        in_specs=(
            P(("shots", "inline"), "xline", None),
            P(("shots", "inline"), "xline", None),
            P(("shots", "inline"), "xline", None),
            P(("shots", "inline"), "xline", None),
            P("inline", "xline", None),
            P("inline", "xline", None),
            P("shots", ("xline", "inline")),
            P(("xline", "inline"), None),
            P(("xline", "inline"), None),
            P("shots"),
            P("shots", None),
        ),
        out_specs=(
            P(("shots", "xline"), "inline", None),
            P(("shots", "inline"), "xline", None),
            P(("shots", "inline"), "xline", None),
        ),
        check_vma=False,
    )
```
